128 devices in a mesh: ctx: 32 (over x_hi, z, y), ch: 4 (over x_lo, core).
Axes of the slice: x: 4 (x_hi: 2, x_lo: 2; x = x_hi * 2 + x_lo), y: 4, z: 4, core: 2. Of those that a mesh axis runs over, the one named last changes fastest.
Arguments:
- prefix_values: bfloat16 [16384, 4096], P('ctx', 'ch'), may hold values from -6 to 6
- suffix_values: bfloat16 [32768, 4096], P('ctx', 'ch'), may hold values from -6 to 6
- suffix_gates: bfloat16 [32768, 4096], P('ctx', 'ch'), may hold values from -6 to 6
- rates: float32 [16, 4096], P(None, 'ch'), may hold values from 4.06901042e-06 to 0.041666667
- residues: float32 [16, 4096], P(None, 'ch'), may hold values from -1.5 to 1.5
- norm_gain: float32 [4096], P('ch'), may hold values from 0.5 to 1.5
- block_order: int32 [64], replicated, may hold values from 0 to 63, each once
- prefix_blocks: int32 [1], replicated, may hold values from 1 to 32
Outputs:
- mixed: bfloat16 [32768, 4096], P('ctx', 'ch')
The draws below stay inside these ranges and needn't reach their ends.
Inputs may be any that keep to these rules, and one draw needn't show every extreme that they name: `block_order`: each number once.
All inputs are finite; a program needn't handle non-finite values.
Results may differ from the reference program's by a relative error of at most 0.0085.
Values may be sent and summed in bfloat16 or wider, within the bound.
A program may use at most 192 MiB of HBM per device.

```python
import math
import jax
import jax.numpy as jnp
from jax import lax

CHN = 4096
MODES = 16
BLK = 512
NPRE = 16384
NBLK = 64
NSUF = 32768
N_CTX = 32


def draw_rates(key, part):
    key = jax.random.fold_in(key, 11)
    key_pick, key_slow, key_fast = jax.random.split(key, 3)
    total = 3.0 * N_CTX * BLK
    share = 0.5
    pick = jax.random.uniform(key_pick, (MODES, CHN), jnp.float32) < share
    slow = jnp.exp(jax.random.uniform(key_slow, (MODES, CHN), jnp.float32, math.log(0.2 / total), math.log(2.0 / total)))
    fast = jnp.exp(jax.random.uniform(key_fast, (MODES, CHN), jnp.float32, math.log(2.0 / total), math.log(1.0 / 24.0)))
    return jnp.where(pick, slow, fast).astype(jnp.float32)


def levels(key, shape, cuts, low, high):
    factor_of = 1.0
    for position, parts in cuts:
        steps = jax.random.uniform(jax.random.fold_in(jax.random.fold_in(key, 6), position), (parts,), jnp.float32, low / len(cuts), high / len(cuts))
        factor_of = factor_of * jnp.repeat(jnp.exp(steps), shape[position] // parts).reshape((-1,) + (1,) * (len(shape) - 1 - position))
    return factor_of


def noise(own_key, dims, spread, reach, cuts=(), kind=jnp.bfloat16):
    factor_of = levels(own_key, dims, cuts, -0.22, 0.18) if cuts else 1.0
    result = jax.random.normal(own_key, dims, jnp.float32) * spread * factor_of
    return jnp.minimum(jnp.maximum(result, -reach), reach).astype(kind)


def setup_inputs(seed: int = 0) -> dict:
    streams_of = jax.random.split(jax.random.key(seed), 9)
    return {
        "prefix_values": noise(streams_of[0], (NPRE, CHN), 1.0, 6.0, ((0, 32), (1, 4))),
        "suffix_values": noise(streams_of[1], (NSUF, CHN), 1.0, 6.0, ((0, 32), (1, 4))),
        "suffix_gates": noise(streams_of[2], (NSUF, CHN), 1.0, 6.0, ((0, 32), (1, 4))),
        "rates": draw_rates(jax.random.fold_in(streams_of[8], 71), 0),
        "residues": noise(streams_of[4], (MODES, CHN), 0.25, 1.5, ((1, 4),), jnp.float32),
        "norm_gain": jnp.clip(1.0 + 0.1 * jax.random.normal(streams_of[5], (CHN,), jnp.float32), 0.5, 1.5),
        "block_order": jax.random.permutation(streams_of[6], NBLK).astype(jnp.int32),
        "prefix_blocks": jax.random.randint(streams_of[7], (1,), 1, N_CTX + 1).astype(jnp.int32),
    }


def reference(prefix_values, suffix_values, suffix_gates, rates, residues, norm_gain, block_order, prefix_blocks):
    nblk = 2 * N_CTX
    npre = N_CTX * BLK
    nsuf = nblk * BLK
    total = npre + nsuf
    plen = prefix_blocks[0] * BLK
    rows = jnp.arange(npre, dtype=jnp.int32)
    live = jnp.where((rows < plen)[:, None], prefix_values.astype(jnp.float32), jnp.float32(0.0))
    moved = jnp.roll(live, npre - plen, axis=0)
    slot_of = jnp.argsort(block_order).astype(jnp.int32)
    ordered = suffix_values.reshape(nblk, BLK, CHN)[slot_of].reshape(nsuf, CHN).astype(jnp.float32)
    sequence = jnp.concatenate([moved, ordered], 0)
    coef = residues * jnp.sqrt(2.0 * rates)
    lags = jnp.arange(total, dtype=jnp.float32)
    group = min(256, CHN)
    size = 2 * total

    def one_group(index):
        cols = index * group
        seq = lax.dynamic_slice_in_dim(sequence, cols, group, 1)
        decay = lax.dynamic_slice_in_dim(rates, cols, group, 1)
        amps = lax.dynamic_slice_in_dim(coef, cols, group, 1)

        def add_mode(taps, mode):
            return (taps + amps[mode][None, :] * jnp.exp(-decay[mode][None, :] * lags[:, None]), None)
        taps, _ = lax.scan(add_mode, jnp.zeros((total, group), jnp.float32), jnp.arange(MODES, dtype=jnp.int32))
        spectrum = jnp.fft.rfft(seq, size, axis=0) * jnp.fft.rfft(taps, size, axis=0)
        full = jnp.fft.irfft(spectrum, size, axis=0)
        return full[npre:total].astype(jnp.float32)
    pieces = lax.map(one_group, jnp.arange(CHN // group, dtype=jnp.int32))
    conv = jnp.transpose(pieces, (1, 0, 2)).reshape(nsuf, CHN)
    stored = conv.reshape(nblk, BLK, CHN)[block_order].reshape(nsuf, CHN)
    gated = suffix_gates.astype(jnp.float32) * stored
    scale = lax.rsqrt(lax.optimization_barrier(jnp.mean(gated * gated, axis=1)) + 1e-06)
    return (gated * scale[:, None] * norm_gain[None, :]).astype(jnp.bfloat16)
```

```python
import functools

import jax
import jax.numpy as jnp
import ml_dtypes
import numpy as np
from jax import lax
from jax.experimental import pallas as pl
from jax.experimental.pallas import tpu as pltpu
from jax.sharding import PartitionSpec as P

MESH = pl.DeviceIdType.MESH
F32 = jnp.float32
BF16 = jnp.bfloat16

LEN = 256
ORD = 16
MODES = 16
CTX = 32
CH = 4
CHANS = 1024
TILES = CHANS // 128
RATE_HALF = 1.0 / 48.0
EPS = 1e-6


def series():
    nodes = 64
    angle = np.pi * (np.arange(nodes) + 0.5) / nodes
    rate = RATE_HALF * (1.0 + np.cos(angle))
    values = np.exp(-rate[:, None] * np.arange(LEN)[None, :])
    basis = np.cos(np.arange(ORD)[:, None] * angle[None, :])
    psi = 2.0 / nodes * (basis @ values)
    psi[0] *= 0.5
    return psi


def halves(a):
    high = a.astype(np.float32).astype(ml_dtypes.bfloat16)
    low = (a - high.astype(np.float64)).astype(np.float32).astype(ml_dtypes.bfloat16)
    return high, low


def tables():
    psi = series()
    theta = np.pi / (2 * LEN) * np.outer(2 * np.arange(LEN) + 1, np.arange(LEN))
    forward = np.concatenate([np.cos(theta), -np.sin(theta)], 0)
    inverse = np.concatenate([np.cos(theta).T, -np.sin(theta).T], 1) / LEN
    to_bf16 = lambda a: a.astype(np.float32).astype(ml_dtypes.bfloat16)
    ends = np.concatenate(halves(psi[:, ::-1]), 0)
    th, tl = halves(forward @ psi.T)
    fh, fl = halves(psi.T)
    return (
        ends,
        to_bf16(forward),
        to_bf16(inverse),
        np.concatenate([th, tl, th], 1),
        np.concatenate([fh, fl, fh], 1),
    )


def split(a):
    high = a.astype(BF16)
    low = (a - high.astype(F32)).astype(BF16)
    return high, low


def dot(a, b):
    return jnp.dot(a, b, preferred_element_type=F32)


def kernel(
    order, blocks, prefix, suffix, gates, rates, residues, gain,
    ends_h, forward_h, inverse_h, taps_h, far_h,
    out,
    x, gt, near, outb, rate_v, res_v, gain_v,
    ends, forward, inverse, taps, fart,
    idx_v, idx_s,
    relay, zrel, tt, coef, step1, dec1, dec2, dec2s, pw,
    mid, spec, prod, hr, hi, hb, grel, gb,
    send1, recv1, incoming, send2, recv2, acc, ss, rss,
    sem_small, sem_x, sem_gate, sem_const, sem_idx, sem_out,
    s1, r1, s2, r2, s3, r3,
):
    me = lax.axis_index("ctx")
    mc = lax.axis_index("ch")

    small = [
        pltpu.make_async_copy(rates, rate_v, sem_small.at[0]),
        pltpu.make_async_copy(residues, res_v, sem_small.at[1]),
        pltpu.make_async_copy(ends_h, ends, sem_small.at[2]),
    ]
    for copy in small:
        copy.start()
    xcopies = []
    for c in range(6):
        src = prefix if c < 2 else suffix
        row = (c if c < 2 else c - 2) * LEN
        xcopies.append(
            pltpu.make_async_copy(src.at[pl.ds(row, LEN)], x.at[pl.ds(c * LEN, LEN)], sem_x.at[c])
        )
    for copy in xcopies:
        copy.start()
    consts = [
        pltpu.make_async_copy(a, b, sem_const.at[i])
        for i, (a, b) in enumerate(
            [(taps_h, taps), (forward_h, forward), (inverse_h, inverse), (far_h, fart), (gain, gain_v)]
        )
    ]
    for copy in consts:
        copy.start()
    gate_copy = pltpu.make_async_copy(gates, gt, sem_gate)
    gate_copy.start()

    barrier = pltpu.get_barrier_semaphore()

    @pl.loop(1, CTX)
    def _(r):
        pl.semaphore_signal(
            barrier, inc=1, device_id=(lax.rem(me + r, CTX), mc), device_id_type=MESH
        )

    @pl.loop(1, CH)
    def _(r):
        pl.semaphore_signal(
            barrier, inc=1, device_id=(me, lax.rem(mc + r, CH)), device_id_type=MESH
        )

    lane = lax.broadcasted_iota(jnp.int32, (8, 128), 1)

    def place(s, value):
        row = 3 * (s // 2) + 1 + s % 2
        return jnp.where(lane == order[s], row, value)

    idx_v[...] = lax.fori_loop(0, 2 * CTX, place, jnp.zeros((8, 128), jnp.int32), unroll=8)
    idx_copy = pltpu.make_async_copy(idx_v, idx_s, sem_idx)
    idx_copy.start()

    for copy in small:
        copy.wait()

    def spread(read):
        for g in range(2):
            for l in range(TILES):
                relay[pl.ds(g * 64 + l * 8, 8), :] = read(g, l)

    def mode(m):
        return relay[pl.ds(m // 8 * 64 + m % 8, 8, stride=8), :]

    live = blocks[0]
    gap = jnp.maximum(live - 1 - me, 0).astype(F32) * (2.0 * LEN)
    alive = jnp.where(me < live, 1.0, 0.0).astype(F32)
    spread(lambda g, l: rate_v[pl.ds(g * 8, 8), pl.ds(l * 128, 128)])
    for m in range(MODES):
        rate = mode(m)
        step1[m] = jnp.exp(-rate)
        d1 = jnp.exp(rate * (-1.0 * LEN))
        dec1[m] = d1
        d2 = jnp.exp(rate * (-2.0 * LEN))
        dec2[m] = d2
        dec2s[2 * m] = d2[:4]
        dec2s[2 * m + 1] = d2[4:]
        pw[m] = jnp.exp(rate * -gap) * alive
        coef[m] = jnp.sqrt(2.0 * rate)
        s = rate * (1.0 / RATE_HALF) - 1.0
        older, newer = jnp.ones_like(s), s
        tt[m, 0] = older
        tt[m, 1] = newer
        for k in range(2, ORD):
            older, newer = newer, 2.0 * s * newer - older
            tt[m, k] = newer
    spread(lambda g, l: res_v[pl.ds(g * 8, 8), pl.ds(l * 128, 128)])
    for m in range(MODES):
        coef[m] = coef[m] * mode(m)

    for c in range(6):
        xcopies[c].wait()
        for n in range(4):
            z = dot(ends[...], x[pl.ds(c * LEN, LEN), pl.ds(n * 256, 256)])
            z = z[:ORD] + z[ORD:]
            for g in range(2):
                for h in range(2):
                    zrel[c, pl.ds(g * 64 + (2 * n + h) * 8, 8), :] = z[
                        g * 8 : g * 8 + 8, h * 128 : h * 128 + 128
                    ]

    @pl.loop(0, MODES)
    def _(m):
        e = [None] * 6
        for k in range(ORD):
            t = tt[m, k]
            for c in range(6):
                term = t * zrel[c, pl.ds(k // 8 * 64 + k % 8, 8, stride=8), :]
                e[c] = term if k == 0 else e[c] + term
        d1 = dec1[m]
        mid[0, m] = e[2]
        mid[1, m] = e[4]
        full = [(e[0] * d1 + e[1]) * pw[m], e[2] * d1 + e[3], e[4] * d1 + e[5]]
        for j in range(3):
            send1[2 * m, j] = full[j][:4]
            send1[2 * m + 1, j] = full[j][4:]

    pl.semaphore_wait(barrier, CTX - 1 + CH - 1)

    @pl.loop(1, CTX)
    def _(r):
        to = lax.rem(me + r, CTX)
        pltpu.make_async_remote_copy(
            src_ref=send1.at[to], dst_ref=recv1.at[pl.ds(3 * me, 3)], send_sem=s1, recv_sem=r1,
            device_id=(to, mc), device_id_type=MESH,
        ).start()

    for j in range(3):
        recv1[3 * me + j] = send1[me, j]

    for copy in consts:
        copy.wait()

    def natural(values, write):
        for k in range(ORD):
            grel[pl.ds(k * 8, 8), :] = values(k)
        for l in range(TILES):
            high, low = split(grel[pl.ds(l, ORD, stride=8), :])
            write(l, jnp.concatenate([high, high, low], 0))

    def tap_term(k):
        total = tt[0, k] * coef[0]
        for m in range(1, MODES):
            total = total + tt[m, k] * coef[m]
        return total

    def put_taps(l, rows):
        hb[:, pl.ds(l * 128, 128)] = rows

    natural(tap_term, put_taps)

    @pl.loop(0, 4)
    def _(n):
        cols = pl.ds(pl.multiple_of(n * 256, 256), 256)
        both = dot(taps[...], hb[:, cols])
        hr[:, cols] = both[:LEN]
        hi[:, cols] = both[LEN:]

    def near_tile(i):
        c, n = i // 4, i % 4
        cols = pl.ds(pl.multiple_of(n * 256, 256), 256)
        rows = pl.ds(pl.multiple_of(c * LEN, LEN), LEN)
        spec[...] = dot(forward[...], x[pl.ds(pl.multiple_of((c + 2) * LEN, LEN), LEN), cols])
        xr, xi = spec[pl.ds(0, LEN), :], spec[pl.ds(LEN, LEN), :]
        tr, ti = hr[:, cols], hi[:, cols]
        prod[pl.ds(0, LEN), :] = (xr * tr - xi * ti).astype(BF16)
        prod[pl.ds(LEN, LEN), :] = (xr * ti + xi * tr).astype(BF16)
        near[rows, cols] = dot(inverse[...], prod[...])

    pl.loop(0, 8)(near_tile)

    pltpu.make_async_copy(
        recv1.at[pl.ds(0, 3 * (CTX - 1))], recv1.at[pl.ds(0, 3 * (CTX - 1))], r1
    ).wait()
    idx_copy.wait()
    parts = [recv1[3 * i] for i in range(4)]
    for i in range(4, CTX):
        parts[i % 4] = parts[i % 4] + recv1[3 * i]
    state = (parts[0] + parts[1]) + (parts[2] + parts[3])
    a = dec2s[me]
    aa = a * a
    for j in range(CTX):
        first, second = [recv1[idx_s[0, 2 * j + q]] for q in range(2)]
        incoming[2 * j] = state
        incoming[2 * j + 1] = a * state + first
        state = aa * state + (a * first + second)
    for s in range(2 * CTX):
        send2[s // 2, s % 2] = incoming[order[s]]

    @pl.loop(1, CTX)
    def _(r):
        to = lax.rem(me + r, CTX)
        pltpu.make_async_remote_copy(
            src_ref=send2.at[to], dst_ref=recv2.at[me], send_sem=s2, recv_sem=r2,
            device_id=(to, mc), device_id_type=MESH,
        ).start()

    for q in range(2):
        recv2[me, q] = send2[me, q]

    pl.loop(8, 16)(near_tile)

    gate_copy.wait()
    pltpu.make_async_copy(recv2.at[pl.ds(0, CTX - 1)], recv2.at[pl.ds(0, CTX - 1)], r2).wait()

    @pl.loop(0, MODES)
    def _(m):
        scale = coef[m] * step1[m]
        for q in range(2):
            state = jnp.concatenate([recv2[2 * m, q], recv2[2 * m + 1, q]], 0)
            spread_g = state * scale
            zrel[2 * q, pl.ds(pl.multiple_of(m * 8, 8), 8), :] = spread_g
            zrel[2 * q + 1, pl.ds(pl.multiple_of(m * 8, 8), 8), :] = (
                state * dec1[m] + mid[q, m]
            ) * scale

    @pl.loop(0, ORD)
    def _(k):
        g = [None] * 4
        for m in range(MODES):
            t = tt[m, k]
            for c in range(4):
                term = t * zrel[c, pl.ds(m * 8, 8), :]
                g[c] = term if m == 0 else g[c] + term
        for c in range(4):
            gb[c, pl.ds(pl.multiple_of(k * 8, 8), 8), :] = g[c]

    ones = jnp.ones((8, 128), BF16)
    for c in range(4):
        rows = pl.ds(c * LEN, LEN)

        def put_far(l, value):
            hb[:, pl.ds(l * 128, 128)] = value

        natural(lambda k: gb[c, pl.ds(k * 8, 8), :], put_far)
        for n in range(4):
            cols = pl.ds(n * 256, 256)
            value = near[rows, cols] + dot(fart[...], hb[:, cols])
            value = value * gt[rows, cols].astype(F32)
            near[rows, cols] = value
            square = value * value
            square = square[:, :128] + square[:, 128:]
            acc[...] = square if n == 0 else acc[...] + square
        high, low = split(acc[...])
        dims = (((1,), (1,)), ((), ()))
        sums = lax.dot_general(ones, high, dims, preferred_element_type=F32)
        sums = sums + lax.dot_general(ones, low, dims, preferred_element_type=F32)
        ss[pl.ds(2 * c, 1), :] = sums[:1, :128]
        ss[pl.ds(2 * c + 1, 1), :] = sums[:1, 128:]

    @pl.loop(1, CH)
    def _(r):
        to = lax.rem(mc + r, CH)
        pltpu.make_async_remote_copy(
            src_ref=ss, dst_ref=rss.at[mc], send_sem=s3, recv_sem=r3,
            device_id=(me, to), device_id_type=MESH,
        ).start()

    rss[mc] = ss[...]
    pltpu.make_async_copy(rss.at[pl.ds(0, CH - 1)], rss.at[pl.ds(0, CH - 1)], r3).wait()
    total = (rss[0] + rss[1]) + (rss[2] + rss[3])
    factor = lax.rsqrt(total * (1.0 / (CH * CHANS)) + EPS)
    for g in range(8):
        rows = pl.ds(g * 128, 128)
        column = jnp.transpose(jnp.broadcast_to(factor[g : g + 1, :], (128, 128)))
        for l in range(TILES):
            cols = pl.ds(l * 128, 128)
            outb[rows, cols] = (near[rows, cols] * column * gain_v[:, cols]).astype(BF16)
        pltpu.make_async_copy(outb.at[rows], out.at[rows], sem_out.at[g]).start()

    for g in range(8):
        rows = pl.ds(g * 128, 128)
        pltpu.make_async_copy(outb.at[rows], out.at[rows], sem_out.at[g]).wait()
    pltpu.make_async_copy(send1.at[pl.ds(0, CTX - 1)], send1.at[pl.ds(0, CTX - 1)], s1).wait()
    pltpu.make_async_copy(send2.at[pl.ds(0, CTX - 1)], send2.at[pl.ds(0, CTX - 1)], s2).wait()
    pltpu.make_async_copy(rss.at[pl.ds(0, CH - 1)], rss.at[pl.ds(0, CH - 1)], s3).wait()


def local(prefix, suffix, gates, rates, residues, gain, order, blocks):
    consts = [jnp.asarray(a) for a in tables()]
    hbm = pl.BlockSpec(memory_space=pl.ANY)
    smem = pl.BlockSpec(memory_space=pltpu.SMEM)
    vmem = pltpu.VMEM
    dma = pltpu.SemaphoreType.DMA
    scratch = [
        vmem((6 * LEN, CHANS), BF16),
        vmem((4 * LEN, CHANS), BF16),
        vmem((4 * LEN, CHANS), F32),
        vmem((4 * LEN, CHANS), BF16),
        vmem((MODES, CHANS), F32),
        vmem((MODES, CHANS), F32),
        vmem((1, CHANS), F32),
        vmem((2 * ORD, LEN), BF16),
        vmem((2 * LEN, LEN), BF16),
        vmem((LEN, 2 * LEN), BF16),
        vmem((2 * LEN, 3 * ORD), BF16),
        vmem((LEN, 3 * ORD), BF16),
        vmem((8, 128), jnp.int32),
        pltpu.SMEM((8, 128), jnp.int32),
        vmem((128, 128), F32),
        vmem((6, 128, 128), F32),
        vmem((MODES, ORD, 8, 128), F32),
        vmem((MODES, 8, 128), F32),
        vmem((MODES, 8, 128), F32),
        vmem((MODES, 8, 128), F32),
        vmem((MODES, 8, 128), F32),
        vmem((2 * MODES, 4, 128), F32),
        vmem((MODES, 8, 128), F32),
        vmem((2, MODES, 8, 128), F32),
        vmem((2 * LEN, 256), F32),
        vmem((2 * LEN, 256), BF16),
        vmem((LEN, CHANS), F32),
        vmem((LEN, CHANS), F32),
        vmem((3 * ORD, CHANS), BF16),
        vmem((128, 128), F32),
        vmem((4, 128, 128), F32),
        vmem((CTX, 3, 4, 128), F32),
        vmem((3 * CTX, 4, 128), F32),
        vmem((2 * CTX, 4, 128), F32),
        vmem((CTX, 2, 4, 128), F32),
        vmem((CTX, 2, 4, 128), F32),
        vmem((LEN, 128), F32),
        vmem((8, 128), F32),
        vmem((CH, 8, 128), F32),
        dma((3,)),
        dma((6,)),
        dma,
        dma((5,)),
        dma,
        dma((8,)),
        dma, dma, dma, dma, dma, dma,
    ]
    return pl.pallas_call(
        kernel,
        out_shape=jax.ShapeDtypeStruct((4 * LEN, CHANS), BF16),
        in_specs=[smem, smem] + [hbm] * 11,
        out_specs=hbm,
        scratch_shapes=scratch,
        compiler_params=pltpu.CompilerParams(
            collective_id=0, has_side_effects=True, vmem_limit_bytes=48 * 1024 * 1024
        ),
        cost_estimate=pl.CostEstimate(
            flops=6_000_000_000, bytes_accessed=8_000_000, transcendentals=100_000
        ),
    )(order, blocks, prefix, suffix, gates, rates, residues, gain[None, :], *consts)


def solution(mesh):
    return jax.shard_map(
        local,
        mesh=mesh,
        in_specs=(
            P("ctx", "ch"),
            P("ctx", "ch"),
            P("ctx", "ch"),
            P(None, "ch"),
            P(None, "ch"),
            P("ch"),
            P(),
            P(),
        ),
        out_specs=P("ctx", "ch"),
        check_vma=False,
    )
```

```python
import functools

import jax
import jax.numpy as jnp
import ml_dtypes
import numpy as np
from jax import lax
from jax.experimental import pallas as pl
from jax.experimental.pallas import tpu as pltpu
from jax.sharding import PartitionSpec as P

MESH = pl.DeviceIdType.MESH
F32 = jnp.float32
BF16 = jnp.bfloat16

LEN = 256
ORD = 16
MODES = 16
CTX = 32
CH = 4
CHANS = 1024
TILES = CHANS // 128
RATE_HALF = 1.0 / 48.0
EPS = 1e-6


def series():
    nodes = 64
    angle = np.pi * (np.arange(nodes) + 0.5) / nodes
    rate = RATE_HALF * (1.0 + np.cos(angle))
    values = np.exp(-rate[:, None] * np.arange(LEN)[None, :])
    basis = np.cos(np.arange(ORD)[:, None] * angle[None, :])
    psi = 2.0 / nodes * (basis @ values)
    psi[0] *= 0.5
    return psi


def halves(a):
    high = a.astype(np.float32).astype(ml_dtypes.bfloat16)
    low = (a - high.astype(np.float64)).astype(np.float32).astype(ml_dtypes.bfloat16)
    return high, low


def tables():
    psi = series()
    theta = np.pi / (2 * LEN) * np.outer(2 * np.arange(LEN) + 1, np.arange(LEN))
    forward = np.concatenate([np.cos(theta), -np.sin(theta)], 0)
    inverse = np.concatenate([np.cos(theta).T, -np.sin(theta).T], 1) / LEN
    to_bf16 = lambda a: a.astype(np.float32).astype(ml_dtypes.bfloat16)
    ends = np.concatenate(halves(psi[:, ::-1]), 0)
    th, tl = halves(forward @ psi.T)
    fh, fl = halves(psi.T)
    arrays = (
        ends,
        np.concatenate([th, tl, th], 1),
        to_bf16(forward),
        to_bf16(inverse),
        np.concatenate([fh, fl, fh], 1),
    )
    slabs, places, row = [], [], 0
    for a in arrays:
        a = np.pad(a, ((0, 0), (0, -a.shape[1] % 128)))
        for col in range(0, a.shape[1], 128):
            slabs.append(a[:, col : col + 128])
            places.append((row, a.shape[0], col))
            row += a.shape[0]
    return np.concatenate(slabs, 0), places


def offsets():
    steps = [(dx, dz, dy) for dx in range(2) for dz in range(4) for dy in range(4)]
    hops = lambda s: 2 * s[0] + min(s[1], 4 - s[1]) + min(s[2], 4 - s[2])
    return sorted(steps[1:], key=hops, reverse=True)


def split(a):
    high = a.astype(BF16)
    low = (a - high.astype(F32)).astype(BF16)
    return high, low


def dot(a, b):
    return jnp.dot(a, b, preferred_element_type=F32)


def kernel(
    places,
    blocks, order_h, prefix, suffix, gates, rates, residues, gain, packed,
    out,
    order, x, gt, near, rate_v, res_v, gain_v,
    ends, forward, inverse, taps, fart,
    idx_v, idx_s,
    relay, zrel, zd, tt, rate_m, coef, step1, dec1, dec2s, pw,
    mid, spec, prod, hr, hi, hb, grel, gm, gb, hf,
    send1, recv1, incoming, send2, recv2, acc, ss, rss,
    sem_small, sem_x, sem_gate, sem_const, sem_idx,
    s1, r1, s2, r2, s3, r3,
):
    me = lax.axis_index("ctx")
    mc = lax.axis_index("ch")

    small = [
        pltpu.make_async_copy(rates, rate_v, sem_small.at[0]),
        pltpu.make_async_copy(residues, res_v, sem_small.at[1]),
        pltpu.make_async_copy(order_h, order, sem_small.at[2]),
    ]
    targets = [ends] * 2 + [taps] + [forward] * 2 + [inverse] * 4 + [fart]
    consts = [
        pltpu.make_async_copy(
            packed.at[pl.ds(row, count)], target.at[:, pl.ds(col, 128)], sem_const.at[i]
        )
        for i, ((row, count, col), target) in enumerate(zip(places, targets))
    ]
    consts.append(pltpu.make_async_copy(gain, gain_v, sem_const.at[len(consts)]))
    for copy in small + consts[:2]:
        copy.start()
    xcopies = []
    for c in range(6):
        src = prefix if c < 2 else suffix
        row = (c if c < 2 else c - 2) * LEN
        xcopies.append(
            pltpu.make_async_copy(src.at[pl.ds(row, LEN)], x.at[pl.ds(c * LEN, LEN)], sem_x.at[c])
        )
    for copy in xcopies:
        copy.start()

    barrier = pltpu.get_barrier_semaphore()
    xs = [lax.rem(me // 16 + d, 2) * 16 for d in range(2)]
    zs = [lax.rem(me // 4 + d, 4) * 4 for d in range(4)]
    ys = [lax.rem(me + d, 4) for d in range(4)]
    peers = [xs[dx] + zs[dz] + ys[dy] for dx, dz, dy in offsets()]
    others = [lax.rem(mc + r, CH) for r in (2, 3, 1)]
    for to in peers:
        pl.semaphore_signal(barrier, inc=1, device_id=(to, mc), device_id_type=MESH)
    for to in others:
        pl.semaphore_signal(barrier, inc=1, device_id=(me, to), device_id_type=MESH)

    for copy in consts[2:]:
        copy.start()
    gate_copy = pltpu.make_async_copy(gates, gt, sem_gate)
    gate_copy.start()

    for copy in small:
        copy.wait()

    def spread(read):
        for g in range(2):
            for l in range(TILES):
                relay[pl.ds(g * 64 + l * 8, 8), :] = read(g, l)

    def mode(m):
        return relay[pl.ds(m // 8 * 64 + m % 8, 8, stride=8), :]

    live = blocks[0]
    gap = jnp.maximum(live - 1 - me, 0).astype(F32) * (2.0 * LEN)
    alive = jnp.where(me < live, 1.0, 0.0).astype(F32)
    spread(lambda g, l: rate_v[pl.ds(g * 8, 8), pl.ds(l * 128, 128)])
    for m in range(MODES):
        rate = mode(m)
        rate_m[m] = rate
        dec1[m] = jnp.exp(rate * (-1.0 * LEN))
        pw[m] = jnp.exp(rate * -gap) * alive
        s = rate * (1.0 / RATE_HALF) - 1.0
        older, newer = jnp.ones_like(s), s
        tt[m, 0] = older
        tt[m, 1] = newer
        for k in range(2, ORD):
            older, newer = newer, 2.0 * s * newer - older
            tt[m, k] = newer

    for copy in consts[:2]:
        copy.wait()
    for c in range(6):
        xcopies[c].wait()
        for n in range(4):
            z = dot(ends[...], x[pl.ds(c * LEN, LEN), pl.ds(n * 256, 256)])
            z = z[:ORD] + z[ORD:]
            for g in range(2):
                for h in range(2):
                    zrel[c, pl.ds(g * 64 + (2 * n + h) * 8, 8), :] = z[
                        g * 8 : g * 8 + 8, h * 128 : h * 128 + 128
                    ]

    for c in range(6):
        for k in range(ORD):
            zd[c, k] = zrel[c, pl.ds(k // 8 * 64 + k % 8, 8, stride=8), :]

    @pl.loop(0, MODES, step=4)
    def _(first):
        e = [[None] * 6 for _ in range(4)]
        for k in range(ORD):
            z = [zd[c, k] for c in range(6)]
            for i in range(4):
                t = tt[first + i, k]
                for c in range(6):
                    e[i][c] = t * z[c] if k == 0 else e[i][c] + t * z[c]
        for i in range(4):
            m = first + i
            d1 = dec1[m]
            mid[0, m] = e[i][2]
            mid[1, m] = e[i][4]
            full = [
                (e[i][0] * d1 + e[i][1]) * pw[m],
                e[i][2] * d1 + e[i][3],
                e[i][4] * d1 + e[i][5],
            ]
            for j in range(3):
                send1[2 * m, j] = full[j][:4]
                send1[2 * m + 1, j] = full[j][4:]

    pl.semaphore_wait(barrier, CTX - 1 + CH - 1)

    for to in peers:
        pltpu.make_async_remote_copy(
            src_ref=send1.at[to], dst_ref=recv1.at[pl.ds(3 * me, 3)], send_sem=s1, recv_sem=r1,
            device_id=(to, mc), device_id_type=MESH,
        ).start()

    for j in range(3):
        recv1[3 * me + j] = send1[me, j]

    lane = lax.broadcasted_iota(jnp.int32, (8, 128), 1)

    def place(s, value):
        row = 3 * (s // 2) + 1 + s % 2
        return jnp.where(lane == order[s], row, value)

    idx_v[...] = lax.fori_loop(0, 2 * CTX, place, jnp.zeros((8, 128), jnp.int32), unroll=8)
    idx_copy = pltpu.make_async_copy(idx_v, idx_s, sem_idx)
    idx_copy.start()

    spread(lambda g, l: res_v[pl.ds(g * 8, 8), pl.ds(l * 128, 128)])
    for m in range(MODES):
        rate = rate_m[m]
        step1[m] = jnp.exp(-rate)
        d2 = jnp.exp(rate * (-2.0 * LEN))
        dec2s[2 * m] = d2[:4]
        dec2s[2 * m + 1] = d2[4:]
        coef[m] = jnp.sqrt(2.0 * rate) * mode(m)

    for copy in consts[2:]:
        copy.wait()

    def natural(tiles, rows):
        for l in range(TILES):
            high, low = split(tiles[pl.ds(l, ORD, stride=8), :])
            rows[:, pl.ds(l * 128, 128)] = jnp.concatenate([high, high, low], 0)

    @pl.loop(0, ORD, step=4)
    def _(first):
        total = [None] * 4
        for m in range(MODES):
            for i in range(4):
                term = tt[m, first + i] * coef[m]
                total[i] = term if m == 0 else total[i] + term
        for i in range(4):
            grel[pl.ds(pl.multiple_of((first + i) * 8, 8), 8), :] = total[i]

    natural(grel, hb)

    @pl.loop(0, 4)
    def _(n):
        cols = pl.ds(pl.multiple_of(n * 256, 256), 256)
        both = dot(taps[:, : 3 * ORD], hb[:, cols])
        hr[:, cols] = both[:LEN]
        hi[:, cols] = both[LEN:]

    def near_chunk(c):
        rows = pl.ds(pl.multiple_of(c * LEN, LEN), LEN)
        xrows = pl.ds(pl.multiple_of((c + 2) * LEN, LEN), LEN)
        cols = [pl.ds(n * 256, 256) for n in range(4)]
        low, high = pl.ds(0, LEN), pl.ds(LEN, LEN)

        def to_spectrum(n):
            spec[n] = dot(forward[...], x[xrows, cols[n]])

        to_spectrum(0)
        for n in range(4):
            if n < 3:
                to_spectrum(n + 1)
            xr, xi = spec[n, low, :], spec[n, high, :]
            tr, ti = hr[:, cols[n]], hi[:, cols[n]]
            prod[n, low, :] = (xr * tr - xi * ti).astype(BF16)
            prod[n, high, :] = (xr * ti + xi * tr).astype(BF16)
            near[rows, cols[n]] = dot(inverse[...], prod[n])

    pl.loop(0, 2)(near_chunk)

    pltpu.make_async_copy(
        recv1.at[pl.ds(0, 3 * (CTX - 1))], recv1.at[pl.ds(0, 3 * (CTX - 1))], r1
    ).wait()
    idx_copy.wait()
    parts = [recv1[3 * i] for i in range(4)]
    for i in range(4, CTX):
        parts[i % 4] = parts[i % 4] + recv1[3 * i]
    state = (parts[0] + parts[1]) + (parts[2] + parts[3])
    a = dec2s[me]
    aa = a * a
    for j in range(CTX):
        first, second = [recv1[idx_s[0, 2 * j + q]] for q in range(2)]
        incoming[2 * j] = state
        incoming[2 * j + 1] = a * state + first
        state = aa * state + (a * first + second)
    for s in range(2 * CTX):
        send2[s // 2, s % 2] = incoming[order[s]]

    for to in peers:
        pltpu.make_async_remote_copy(
            src_ref=send2.at[to], dst_ref=recv2.at[me], send_sem=s2, recv_sem=r2,
            device_id=(to, mc), device_id_type=MESH,
        ).start()

    for q in range(2):
        recv2[me, q] = send2[me, q]

    pl.loop(2, 4)(near_chunk)

    gate_copy.wait()
    pltpu.make_async_copy(recv2.at[pl.ds(0, CTX - 1)], recv2.at[pl.ds(0, CTX - 1)], r2).wait()

    for m in range(MODES):
        scale = coef[m] * step1[m]
        for q in range(2):
            state = jnp.concatenate([recv2[2 * m, q], recv2[2 * m + 1, q]], 0)
            gm[2 * q, m] = state * scale
            gm[2 * q + 1, m] = (state * dec1[m] + mid[q, m]) * scale

    @pl.loop(0, ORD, step=4)
    def _(first):
        g = [[None] * 4 for _ in range(4)]
        for m in range(MODES):
            u = [gm[c, m] for c in range(4)]
            for i in range(4):
                t = tt[m, first + i]
                for c in range(4):
                    g[i][c] = t * u[c] if m == 0 else g[i][c] + t * u[c]
        for i in range(4):
            for c in range(4):
                gb[c, pl.ds(pl.multiple_of((first + i) * 8, 8), 8), :] = g[i][c]

    for c in range(4):
        natural(gb.at[c], hf.at[c])

    ones = jnp.ones((8, 128), BF16)
    for c in range(4):
        rows = pl.ds(c * LEN, LEN)
        for n in range(4):
            cols = pl.ds(n * 256, 256)
            value = near[rows, cols] + dot(fart[:, : 3 * ORD], hf[c, :, cols])
            value = value * gt[rows, cols].astype(F32)
            near[rows, cols] = value
            square = value * value
            square = square[:, :128] + square[:, 128:]
            acc[c] = square if n == 0 else acc[c] + square
        high, low = split(acc[c])
        dims = (((1,), (1,)), ((), ()))
        sums = lax.dot_general(ones, high, dims, preferred_element_type=F32)
        sums = sums + lax.dot_general(ones, low, dims, preferred_element_type=F32)
        ss[c, pl.ds(0, 1), :] = sums[:1, :128]
        ss[c, pl.ds(1, 1), :] = sums[:1, 128:]
        for to in others:
            pltpu.make_async_remote_copy(
                src_ref=ss.at[c], dst_ref=rss.at[c, mc], send_sem=s3, recv_sem=r3.at[c],
                device_id=(me, to), device_id_type=MESH,
            ).start()
        rss[c, mc] = ss[c]

    for c in range(4):
        three = rss.at[c, pl.ds(0, CH - 1)]
        pltpu.make_async_copy(three, three, r3.at[c]).wait()
        total = (rss[c, 0] + rss[c, 1]) + (rss[c, 2] + rss[c, 3])
        factor = lax.rsqrt(total * (1.0 / (CH * CHANS)) + EPS)
        for g in range(2):
            rows = pl.ds(c * LEN + g * 128, 128)
            column = jnp.transpose(jnp.broadcast_to(factor[g : g + 1, :], (128, 128)))
            for l in range(TILES):
                cols = pl.ds(l * 128, 128)
                out[rows, cols] = (near[rows, cols] * column * gain_v[:, cols]).astype(BF16)

    pltpu.make_async_copy(send1.at[pl.ds(0, CTX - 1)], send1.at[pl.ds(0, CTX - 1)], s1).wait()
    pltpu.make_async_copy(send2.at[pl.ds(0, CTX - 1)], send2.at[pl.ds(0, CTX - 1)], s2).wait()
    pltpu.make_async_copy(rss.at[pl.ds(0, CH - 1)], rss.at[pl.ds(0, CH - 1)], s3).wait()


def local(prefix, suffix, gates, rates, residues, gain, order, blocks):
    packed, places = tables()
    hbm = pl.BlockSpec(memory_space=pltpu.HBM)
    vmem = pltpu.VMEM
    dma = pltpu.SemaphoreType.DMA
    scratch = [
        pltpu.SMEM((2 * CTX,), jnp.int32),
        vmem((6 * LEN, CHANS), BF16),
        vmem((4 * LEN, CHANS), BF16),
        vmem((4 * LEN, CHANS), F32),
        vmem((MODES, CHANS), F32),
        vmem((MODES, CHANS), F32),
        vmem((1, CHANS), F32),
        vmem((2 * ORD, LEN), BF16),
        vmem((2 * LEN, LEN), BF16),
        vmem((LEN, 2 * LEN), BF16),
        vmem((2 * LEN, 128), BF16),
        vmem((LEN, 128), BF16),
        vmem((8, 128), jnp.int32),
        pltpu.SMEM((8, 128), jnp.int32),
        vmem((128, 128), F32),
        vmem((6, 128, 128), F32),
        vmem((6, ORD, 8, 128), F32),
        vmem((MODES, ORD, 8, 128), F32),
        vmem((MODES, 8, 128), F32),
        vmem((MODES, 8, 128), F32),
        vmem((MODES, 8, 128), F32),
        vmem((MODES, 8, 128), F32),
        vmem((2 * MODES, 4, 128), F32),
        vmem((MODES, 8, 128), F32),
        vmem((2, MODES, 8, 128), F32),
        vmem((4, 2 * LEN, 256), F32),
        vmem((4, 2 * LEN, 256), BF16),
        vmem((LEN, CHANS), F32),
        vmem((LEN, CHANS), F32),
        vmem((3 * ORD, CHANS), BF16),
        vmem((128, 128), F32),
        vmem((4, MODES, 8, 128), F32),
        vmem((4, 128, 128), F32),
        vmem((4, 3 * ORD, CHANS), BF16),
        vmem((CTX, 3, 4, 128), F32),
        vmem((3 * CTX, 4, 128), F32),
        vmem((2 * CTX, 4, 128), F32),
        vmem((CTX, 2, 4, 128), F32),
        vmem((CTX, 2, 4, 128), F32),
        vmem((4, LEN, 128), F32),
        vmem((4, 2, 128), F32),
        vmem((4, CH, 2, 128), F32),
        dma((3,)),
        dma((6,)),
        dma,
        dma((len(places) + 1,)),
        dma,
        dma, dma, dma, dma, dma, dma((4,)),
    ]
    operands = (
        order, prefix, suffix, gates, rates, residues, gain[None, :], jnp.asarray(packed)
    )
    return pl.pallas_call(
        functools.partial(kernel, places),
        out_shape=pltpu.VMEM((4 * LEN, CHANS), BF16),
        in_specs=[pl.BlockSpec(memory_space=pltpu.SMEM)] + [hbm] * 8,
        out_specs=pl.BlockSpec(memory_space=pltpu.VMEM),
        scratch_shapes=scratch,
        compiler_params=pltpu.CompilerParams(
            collective_id=0, has_side_effects=True, vmem_limit_bytes=48 * 1024 * 1024
        ),
        cost_estimate=pl.CostEstimate(
            flops=6_000_000_000, bytes_accessed=8_000_000, transcendentals=100_000
        ),
    )(blocks, *(pltpu.with_memory_space_constraint(a, pltpu.HBM) for a in operands))


def solution(mesh):
    return jax.shard_map(
        local,
        mesh=mesh,
        in_specs=(
            P("ctx", "ch"),
            P("ctx", "ch"),
            P("ctx", "ch"),
            P(None, "ch"),
            P(None, "ch"),
            P("ch"),
            P(),
            P(),
        ),
        out_specs=P("ctx", "ch"),
        check_vma=False,
    )
```

```python
import functools

import jax
import jax.numpy as jnp
import ml_dtypes
import numpy as np
from jax import lax
from jax.experimental import pallas as pl
from jax.experimental.pallas import tpu as pltpu
from jax.sharding import PartitionSpec as P

MESH = pl.DeviceIdType.MESH
F32 = jnp.float32
BF16 = jnp.bfloat16

LEN = 256
ORD = 16
MODES = 16
CTX = 32
CH = 4
CHANS = 1024
TILES = CHANS // 128
RATE_HALF = 1.0 / 48.0
EPS = 1e-6


def series():
    nodes = 64
    angle = np.pi * (np.arange(nodes) + 0.5) / nodes
    rate = RATE_HALF * (1.0 + np.cos(angle))
    values = np.exp(-rate[:, None] * np.arange(LEN)[None, :])
    basis = np.cos(np.arange(ORD)[:, None] * angle[None, :])
    psi = 2.0 / nodes * (basis @ values)
    psi[0] *= 0.5
    return psi


def halves(a):
    high = a.astype(np.float32).astype(ml_dtypes.bfloat16)
    low = (a - high.astype(np.float64)).astype(np.float32).astype(ml_dtypes.bfloat16)
    return high, low


def tables():
    psi = series()
    theta = np.pi / (2 * LEN) * np.outer(2 * np.arange(LEN) + 1, np.arange(LEN))
    forward = np.concatenate([np.cos(theta), -np.sin(theta)], 0)
    inverse = np.concatenate([np.cos(theta).T, -np.sin(theta).T], 1) / LEN
    to_bf16 = lambda a: a.astype(np.float32).astype(ml_dtypes.bfloat16)
    ends = np.concatenate(halves(psi[:, ::-1]), 0)
    th, tl = halves(forward @ psi.T)
    fh, fl = halves(psi.T)
    arrays = (
        ends,
        np.concatenate([th, tl, th], 1),
        to_bf16(forward),
        to_bf16(inverse),
        np.concatenate([fh, fl, fh], 1),
    )
    slabs, places, row = [], [], 0
    for a in arrays:
        a = np.pad(a, ((0, 0), (0, -a.shape[1] % 128)))
        for col in range(0, a.shape[1], 128):
            slabs.append(a[:, col : col + 128])
            places.append((row, a.shape[0], col))
            row += a.shape[0]
    return np.concatenate(slabs, 0), places


def place_of(ctx):
    return ctx // 16, ctx // 4 % 4, ctx % 4


def lateness(ctx):
    x, z, y = place_of(ctx)
    return 1.5 * x + 1.0 * z + 0.85 * y


BY_START = sorted(range(CTX), key=lateness)
SERVERS = BY_START[:16]
PER = MODES // len(SERVERS)


def split(a):
    high = a.astype(BF16)
    low = (a - high.astype(F32)).astype(BF16)
    return high, low


def dot(a, b):
    return jnp.dot(a, b, preferred_element_type=F32)


def kernel(
    places,
    blocks, order_h, prefix, suffix, gates, rates, residues, gain, packed,
    out,
    order, x, gt, near, rate_v, res_v, gain_v,
    ends, forward, inverse, taps, fart,
    idx_v, idx_s,
    relay, zrel, zd, tt, rate_m, coef, step1, dec1, dec2, pw,
    mid, spec, prod, hr, hi, hb, grel, gm, gb, hf,
    send1, recv1, incoming, send2, recv2, acc, ss, rss,
    sem_small, sem_x, sem_gate, sem_const, sem_idx,
    s1, r1, s2, r2, s3, r3,
):
    me = lax.axis_index("ctx")
    mc = lax.axis_index("ch")

    small = [
        pltpu.make_async_copy(rates, rate_v, sem_small.at[0]),
        pltpu.make_async_copy(residues, res_v, sem_small.at[1]),
        pltpu.make_async_copy(order_h, order, sem_small.at[2]),
    ]
    targets = [ends] * 2 + [taps] + [forward] * 2 + [inverse] * 4 + [fart]
    consts = [
        pltpu.make_async_copy(
            packed.at[pl.ds(row, count)], target.at[:, pl.ds(col, 128)], sem_const.at[i]
        )
        for i, ((row, count, col), target) in enumerate(zip(places, targets))
    ]
    consts.append(pltpu.make_async_copy(gain, gain_v, sem_const.at[len(consts)]))
    for copy in small + consts[:2]:
        copy.start()
    xcopies = []
    for c in range(6):
        src = prefix if c < 2 else suffix
        row = (c if c < 2 else c - 2) * LEN
        xcopies.append(
            pltpu.make_async_copy(src.at[pl.ds(row, LEN)], x.at[pl.ds(c * LEN, LEN)], sem_x.at[c])
        )
    for copy in xcopies:
        copy.start()

    barrier = pltpu.get_barrier_semaphore()
    others = [lax.rem(mc + r, CH) for r in (2, 3, 1)]
    serves = functools.reduce(jnp.logical_or, [me == ctx for ctx in SERVERS])
    number = sum(jnp.where(me == ctx, i, 0) for i, ctx in enumerate(SERVERS))
    replies = len(SERVERS) - jnp.where(serves, 1, 0)

    @pl.when(serves)
    def _():
        for to in BY_START:

            @pl.when(me != to)
            def _():
                pl.semaphore_signal(barrier, inc=1, device_id=(to, mc), device_id_type=MESH)

    for to in others:
        pl.semaphore_signal(barrier, inc=1, device_id=(me, to), device_id_type=MESH)

    for copy in consts[2:]:
        copy.start()
    gate_copy = pltpu.make_async_copy(gates, gt, sem_gate)
    gate_copy.start()

    for copy in small:
        copy.wait()

    def spread(read):
        for g in range(2):
            for l in range(TILES):
                relay[pl.ds(g * 64 + l * 8, 8), :] = read(g, l)

    def mode(m):
        return relay[pl.ds(m // 8 * 64 + m % 8, 8, stride=8), :]

    live = blocks[0]
    gap = jnp.maximum(live - 1 - me, 0).astype(F32) * (2.0 * LEN)
    alive = jnp.where(me < live, 1.0, 0.0).astype(F32)
    spread(lambda g, l: rate_v[pl.ds(g * 8, 8), pl.ds(l * 128, 128)])
    for m in range(MODES):
        rate = mode(m)
        rate_m[m] = rate
        dec1[m] = jnp.exp(rate * (-1.0 * LEN))
        pw[m] = jnp.exp(rate * -gap) * alive
        s = rate * (1.0 / RATE_HALF) - 1.0
        older, newer = jnp.ones_like(s), s
        tt[m, 0] = older
        tt[m, 1] = newer
        for k in range(2, ORD):
            older, newer = newer, 2.0 * s * newer - older
            tt[m, k] = newer

    for copy in consts[:2]:
        copy.wait()
    for c in range(6):
        xcopies[c].wait()
        for n in range(4):
            z = dot(ends[...], x[pl.ds(c * LEN, LEN), pl.ds(n * 256, 256)])
            z = z[:ORD] + z[ORD:]
            for g in range(2):
                for h in range(2):
                    zrel[c, pl.ds(g * 64 + (2 * n + h) * 8, 8), :] = z[
                        g * 8 : g * 8 + 8, h * 128 : h * 128 + 128
                    ]

    for c in range(6):
        for k in range(ORD):
            zd[c, k] = zrel[c, pl.ds(k // 8 * 64 + k % 8, 8, stride=8), :]

    @pl.loop(0, MODES, step=4)
    def _(first):
        e = [[None] * 6 for _ in range(4)]
        for k in range(ORD):
            z = [zd[c, k] for c in range(6)]
            for i in range(4):
                t = tt[first + i, k]
                for c in range(6):
                    e[i][c] = t * z[c] if k == 0 else e[i][c] + t * z[c]
        for i in range(4):
            m = first + i
            d1 = dec1[m]
            mid[0, m] = e[i][2]
            mid[1, m] = e[i][4]
            full = [
                (e[i][0] * d1 + e[i][1]) * pw[m],
                e[i][2] * d1 + e[i][3],
                e[i][4] * d1 + e[i][5],
            ]
            for j in range(3):
                send1[m, j] = full[j]

    pl.semaphore_wait(barrier, replies + CH - 1)

    for i, to in enumerate(SERVERS):
        part = send1.at[pl.ds(i * PER, PER)]

        @pl.when(me != to)
        def _():
            pltpu.make_async_remote_copy(
                src_ref=part, dst_ref=recv1.at[me], send_sem=s1, recv_sem=r1,
                device_id=(to, mc), device_id_type=MESH,
            ).start()

        @pl.when(me == to)
        def _():
            recv1[me] = part[...]

    lane = lax.broadcasted_iota(jnp.int32, (8, 128), 1)

    def place(s, value):
        return jnp.where(lane == order[s], s, value)

    idx_v[...] = lax.fori_loop(0, 2 * CTX, place, jnp.zeros((8, 128), jnp.int32), unroll=8)
    idx_copy = pltpu.make_async_copy(idx_v, idx_s, sem_idx)
    idx_copy.start()

    spread(lambda g, l: res_v[pl.ds(g * 8, 8), pl.ds(l * 128, 128)])
    for m in range(MODES):
        rate = rate_m[m]
        step1[m] = jnp.exp(-rate)
        d2 = jnp.exp(rate * (-2.0 * LEN))
        dec2[m] = d2
        coef[m] = jnp.sqrt(2.0 * rate) * mode(m)

    for copy in consts[2:]:
        copy.wait()

    def natural(tiles, rows):
        for l in range(TILES):
            high, low = split(tiles[pl.ds(l, ORD, stride=8), :])
            rows[:, pl.ds(l * 128, 128)] = jnp.concatenate([high, high, low], 0)

    @pl.loop(0, ORD, step=4)
    def _(first):
        total = [None] * 4
        for m in range(MODES):
            for i in range(4):
                term = tt[m, first + i] * coef[m]
                total[i] = term if m == 0 else total[i] + term
        for i in range(4):
            grel[pl.ds(pl.multiple_of((first + i) * 8, 8), 8), :] = total[i]

    natural(grel, hb)

    @pl.loop(0, 4)
    def _(n):
        cols = pl.ds(pl.multiple_of(n * 256, 256), 256)
        both = dot(taps[:, : 3 * ORD], hb[:, cols])
        hr[:, cols] = both[:LEN]
        hi[:, cols] = both[LEN:]

    def near_chunk(c):
        rows = pl.ds(pl.multiple_of(c * LEN, LEN), LEN)
        xrows = pl.ds(pl.multiple_of((c + 2) * LEN, LEN), LEN)
        cols = [pl.ds(n * 256, 256) for n in range(4)]
        low, high = pl.ds(0, LEN), pl.ds(LEN, LEN)

        def to_spectrum(n):
            spec[n] = dot(forward[...], x[xrows, cols[n]])

        to_spectrum(0)
        for n in range(4):
            if n < 3:
                to_spectrum(n + 1)
            xr, xi = spec[n, low, :], spec[n, high, :]
            tr, ti = hr[:, cols[n]], hi[:, cols[n]]
            prod[n, low, :] = (xr * tr - xi * ti).astype(BF16)
            prod[n, high, :] = (xr * ti + xi * tr).astype(BF16)
            near[rows, cols[n]] = dot(inverse[...], prod[n])

    pl.loop(0, 2)(near_chunk)

    idx_copy.wait()

    @pl.when(serves)
    def _():
        first31 = recv1.at[pl.ds(0, CTX - 1)]
        pltpu.make_async_copy(first31, first31, r1).wait()
        for i in range(PER):
            parts = [recv1[c, i, 0] for c in range(4)]
            for c in range(4, CTX):
                parts[c % 4] = parts[c % 4] + recv1[c, i, 0]
            state = (parts[0] + parts[1]) + (parts[2] + parts[3])
            a = dec2[number * PER + i]
            aa = a * a
            for j in range(CTX):
                slots = [idx_s[0, 2 * j + q] for q in range(2)]
                first, second = [recv1[lax.div(slot, 2), i, 1 + lax.rem(slot, 2)] for slot in slots]
                incoming[2 * j] = state
                incoming[2 * j + 1] = a * state + first
                state = aa * state + (a * first + second)
            for s in range(2 * CTX):
                send2[s // 2, i, s % 2] = incoming[order[s]]
        for to in BY_START:

            @pl.when(me != to)
            def _():
                pltpu.make_async_remote_copy(
                    src_ref=send2.at[to], dst_ref=recv2.at[pl.ds(number * PER, PER)],
                    send_sem=s2, recv_sem=r2, device_id=(to, mc), device_id_type=MESH,
                ).start()

        for i in range(PER):
            recv2[number * PER + i] = send2[me, i]

    pl.loop(2, 4)(near_chunk)

    gate_copy.wait()
    @pl.when(serves)
    def _():
        rest = recv2.at[pl.ds(0, MODES - PER)]
        pltpu.make_async_copy(rest, rest, r2).wait()

    @pl.when(jnp.logical_not(serves))
    def _():
        pltpu.make_async_copy(recv2, recv2, r2).wait()


    for m in range(MODES):
        scale = coef[m] * step1[m]
        for q in range(2):
            state = recv2[m, q]
            gm[2 * q, m] = state * scale
            gm[2 * q + 1, m] = (state * dec1[m] + mid[q, m]) * scale

    @pl.loop(0, ORD, step=4)
    def _(first):
        g = [[None] * 4 for _ in range(4)]
        for m in range(MODES):
            u = [gm[c, m] for c in range(4)]
            for i in range(4):
                t = tt[m, first + i]
                for c in range(4):
                    g[i][c] = t * u[c] if m == 0 else g[i][c] + t * u[c]
        for i in range(4):
            for c in range(4):
                gb[c, pl.ds(pl.multiple_of((first + i) * 8, 8), 8), :] = g[i][c]

    for c in range(4):
        natural(gb.at[c], hf.at[c])

    ones = jnp.ones((8, 128), BF16)
    for c in range(4):
        rows = pl.ds(c * LEN, LEN)
        for n in range(4):
            cols = pl.ds(n * 256, 256)
            value = near[rows, cols] + dot(fart[:, : 3 * ORD], hf[c, :, cols])
            value = value * gt[rows, cols].astype(F32)
            near[rows, cols] = value
            square = value * value
            square = square[:, :128] + square[:, 128:]
            acc[c] = square if n == 0 else acc[c] + square
        high, low = split(acc[c])
        dims = (((1,), (1,)), ((), ()))
        sums = lax.dot_general(ones, high, dims, preferred_element_type=F32)
        sums = sums + lax.dot_general(ones, low, dims, preferred_element_type=F32)
        ss[c, pl.ds(0, 1), :] = sums[:1, :128]
        ss[c, pl.ds(1, 1), :] = sums[:1, 128:]
        for to in others:
            pltpu.make_async_remote_copy(
                src_ref=ss.at[c], dst_ref=rss.at[c, mc], send_sem=s3, recv_sem=r3.at[c],
                device_id=(me, to), device_id_type=MESH,
            ).start()
        rss[c, mc] = ss[c]

    for c in range(4):
        three = rss.at[c, pl.ds(0, CH - 1)]
        pltpu.make_async_copy(three, three, r3.at[c]).wait()
        total = (rss[c, 0] + rss[c, 1]) + (rss[c, 2] + rss[c, 3])
        factor = lax.rsqrt(total * (1.0 / (CH * CHANS)) + EPS)
        for g in range(2):
            rows = pl.ds(c * LEN + g * 128, 128)
            column = jnp.transpose(jnp.broadcast_to(factor[g : g + 1, :], (128, 128)))
            for l in range(TILES):
                cols = pl.ds(l * 128, 128)
                out[rows, cols] = (near[rows, cols] * column * gain_v[:, cols]).astype(BF16)

    @pl.when(jnp.logical_not(serves))
    def _():
        pltpu.make_async_copy(send1, send1, s1).wait()

    @pl.when(serves)
    def _():
        rest = send1.at[pl.ds(0, MODES - PER)]
        pltpu.make_async_copy(rest, rest, s1).wait()
        sent = send2.at[pl.ds(0, CTX - 1)]
        pltpu.make_async_copy(sent, sent, s2).wait()

    pltpu.make_async_copy(rss.at[pl.ds(0, CH - 1)], rss.at[pl.ds(0, CH - 1)], s3).wait()


def local(prefix, suffix, gates, rates, residues, gain, order, blocks):
    packed, places = tables()
    hbm = pl.BlockSpec(memory_space=pltpu.HBM)
    vmem = pltpu.VMEM
    dma = pltpu.SemaphoreType.DMA
    scratch = [
        pltpu.SMEM((2 * CTX,), jnp.int32),
        vmem((6 * LEN, CHANS), BF16),
        vmem((4 * LEN, CHANS), BF16),
        vmem((4 * LEN, CHANS), F32),
        vmem((MODES, CHANS), F32),
        vmem((MODES, CHANS), F32),
        vmem((1, CHANS), F32),
        vmem((2 * ORD, LEN), BF16),
        vmem((2 * LEN, LEN), BF16),
        vmem((LEN, 2 * LEN), BF16),
        vmem((2 * LEN, 128), BF16),
        vmem((LEN, 128), BF16),
        vmem((8, 128), jnp.int32),
        pltpu.SMEM((8, 128), jnp.int32),
        vmem((128, 128), F32),
        vmem((6, 128, 128), F32),
        vmem((6, ORD, 8, 128), F32),
        vmem((MODES, ORD, 8, 128), F32),
        vmem((MODES, 8, 128), F32),
        vmem((MODES, 8, 128), F32),
        vmem((MODES, 8, 128), F32),
        vmem((MODES, 8, 128), F32),
        vmem((MODES, 8, 128), F32),
        vmem((MODES, 8, 128), F32),
        vmem((2, MODES, 8, 128), F32),
        vmem((4, 2 * LEN, 256), F32),
        vmem((4, 2 * LEN, 256), BF16),
        vmem((LEN, CHANS), F32),
        vmem((LEN, CHANS), F32),
        vmem((3 * ORD, CHANS), BF16),
        vmem((128, 128), F32),
        vmem((4, MODES, 8, 128), F32),
        vmem((4, 128, 128), F32),
        vmem((4, 3 * ORD, CHANS), BF16),
        vmem((MODES, 3, 8, 128), F32),
        vmem((CTX, PER, 3, 8, 128), F32),
        vmem((2 * CTX, 8, 128), F32),
        vmem((CTX, PER, 2, 8, 128), F32),
        vmem((MODES, 2, 8, 128), F32),
        vmem((4, LEN, 128), F32),
        vmem((4, 2, 128), F32),
        vmem((4, CH, 2, 128), F32),
        dma((3,)),
        dma((6,)),
        dma,
        dma((len(places) + 1,)),
        dma,
        dma, dma, dma, dma, dma, dma((4,)),
    ]
    operands = (
        order, prefix, suffix, gates, rates, residues, gain[None, :], jnp.asarray(packed)
    )
    return pl.pallas_call(
        functools.partial(kernel, places),
        out_shape=pltpu.VMEM((4 * LEN, CHANS), BF16),
        in_specs=[pl.BlockSpec(memory_space=pltpu.SMEM)] + [hbm] * 8,
        out_specs=pl.BlockSpec(memory_space=pltpu.VMEM),
        scratch_shapes=scratch,
        compiler_params=pltpu.CompilerParams(
            collective_id=0, has_side_effects=True, vmem_limit_bytes=48 * 1024 * 1024
        ),
        cost_estimate=pl.CostEstimate(
            flops=6_000_000_000, bytes_accessed=8_000_000, transcendentals=100_000
        ),
    )(blocks, *(pltpu.with_memory_space_constraint(a, pltpu.HBM) for a in operands))


def solution(mesh):
    return jax.shard_map(
        local,
        mesh=mesh,
        in_specs=(
            P("ctx", "ch"),
            P("ctx", "ch"),
            P("ctx", "ch"),
            P(None, "ch"),
            P(None, "ch"),
            P("ch"),
            P(),
            P(),
        ),
        out_specs=P("ctx", "ch"),
        check_vma=False,
    )
```

```python
import functools

import jax
import jax.numpy as jnp
import ml_dtypes
import numpy as np
from jax import lax
from jax.experimental import pallas as pl
from jax.experimental.pallas import tpu as pltpu
from jax.sharding import PartitionSpec as P

MESH = pl.DeviceIdType.MESH
F32 = jnp.float32
BF16 = jnp.bfloat16

LEN = 256
ORD = 16
MODES = 16
CTX = 32
CH = 4
CHANS = 1024
TILES = CHANS // 128
RATE_HALF = 1.0 / 48.0
EPS = 1e-6


def series():
    nodes = 64
    angle = np.pi * (np.arange(nodes) + 0.5) / nodes
    rate = RATE_HALF * (1.0 + np.cos(angle))
    values = np.exp(-rate[:, None] * np.arange(LEN)[None, :])
    basis = np.cos(np.arange(ORD)[:, None] * angle[None, :])
    psi = 2.0 / nodes * (basis @ values)
    psi[0] *= 0.5
    return psi


def halves(a):
    high = a.astype(np.float32).astype(ml_dtypes.bfloat16)
    low = (a - high.astype(np.float64)).astype(np.float32).astype(ml_dtypes.bfloat16)
    return high, low


def tables():
    psi = series()
    theta = np.pi / (2 * LEN) * np.outer(2 * np.arange(LEN) + 1, np.arange(LEN))
    forward = np.concatenate([np.cos(theta), -np.sin(theta)], 0)
    inverse = np.concatenate([np.cos(theta).T, -np.sin(theta).T], 1) / LEN
    to_bf16 = lambda a: a.astype(np.float32).astype(ml_dtypes.bfloat16)
    ends = np.concatenate(halves(psi[:, ::-1]), 0)
    th, tl = halves(forward @ psi.T)
    fh, fl = halves(psi.T)
    arrays = (
        ends,
        np.concatenate([th, tl, th], 1),
        to_bf16(forward),
        to_bf16(inverse),
        np.concatenate([fh, fl, fh], 1),
    )
    slabs, places, row = [], [], 0
    for a in arrays:
        a = np.pad(a, ((0, 0), (0, -a.shape[1] % 128)))
        for col in range(0, a.shape[1], 128):
            slabs.append(a[:, col : col + 128])
            places.append((row, a.shape[0], col))
            row += a.shape[0]
    return np.concatenate(slabs, 0), places


def place_of(ctx):
    return ctx // 16, ctx // 4 % 4, ctx % 4


def lateness(ctx):
    x, z, y = place_of(ctx)
    return 1.5 * x + 1.0 * z + 0.85 * y


BY_START = sorted(range(CTX), key=lateness)
SERVERS = BY_START[:MODES]


def split(a):
    high = a.astype(BF16)
    low = (a - high.astype(F32)).astype(BF16)
    return high, low


def dot(a, b):
    return jnp.dot(a, b, preferred_element_type=F32)


def kernel(
    places,
    blocks, order_h, prefix, suffix, gates, rates, residues, gain, packed,
    out,
    order, x, gt, near, rate_v, res_v, gain_v,
    ends, forward, inverse, taps, fart,
    idx_v, idx_s,
    relay, zrel, zd, tt, rate_m, coef, step1, dec1, dec2, pw,
    mid, spec, prod, hr, hi, hb, grel, gm, gb, hf,
    send1, recv1, ends_of, incoming, send2, recv2, acc, ss, rss,
    sem_small, sem_x, sem_gate, sem_const, sem_idx,
    s1, r1, s2, r2, s3, r3,
):
    me = lax.axis_index("ctx")
    mc = lax.axis_index("ch")

    small = [
        pltpu.make_async_copy(rates, rate_v, sem_small.at[0]),
        pltpu.make_async_copy(residues, res_v, sem_small.at[1]),
        pltpu.make_async_copy(order_h, order, sem_small.at[2]),
        pltpu.make_async_copy(gain, gain_v, sem_small.at[3]),
    ]
    targets = [ends] * 2 + [taps] + [forward] * 2 + [inverse] * 4 + [fart]
    consts = [
        pltpu.make_async_copy(
            packed.at[pl.ds(row, count)], target.at[:, pl.ds(col, 128)], sem_const.at[i]
        )
        for i, ((row, count, col), target) in enumerate(zip(places, targets))
    ]
    xcopies = [
        pltpu.make_async_copy(prefix, x.at[pl.ds(0, 2 * LEN)], sem_x.at[0]),
        pltpu.make_async_copy(
            suffix.at[pl.ds(0, 2 * LEN)], x.at[pl.ds(2 * LEN, 2 * LEN)], sem_x.at[1]
        ),
        pltpu.make_async_copy(
            suffix.at[pl.ds(2 * LEN, 2 * LEN)], x.at[pl.ds(4 * LEN, 2 * LEN)], sem_x.at[2]
        ),
    ]
    gate_copy = pltpu.make_async_copy(gates, gt, sem_gate)
    for copy in small[:1] + consts[:2] + xcopies:
        copy.start()

    barrier = pltpu.get_barrier_semaphore()
    others = [lax.rem(mc + r, CH) for r in (2, 3, 1)]
    serves = functools.reduce(jnp.logical_or, [me == ctx for ctx in SERVERS])
    number = sum(jnp.where(me == ctx, i, 0) for i, ctx in enumerate(SERVERS))
    replies = len(SERVERS) - jnp.where(serves, 1, 0)

    @pl.when(serves)
    def _():
        for to in BY_START:

            @pl.when(me != to)
            def _():
                pl.semaphore_signal(barrier, inc=1, device_id=(to, mc), device_id_type=MESH)

    for to in others:
        pl.semaphore_signal(barrier, inc=1, device_id=(me, to), device_id_type=MESH)

    small[0].wait()

    def spread(read):
        for g in range(2):
            for l in range(TILES):
                relay[pl.ds(g * 64 + l * 8, 8), :] = read(g, l)

    def mode(m):
        return relay[pl.ds(m // 8 * 64 + m % 8, 8, stride=8), :]

    live = blocks[0]
    gap = jnp.maximum(live - 1 - me, 0).astype(F32) * (2.0 * LEN)
    alive = jnp.where(me < live, 1.0, 0.0).astype(F32)
    spread(lambda g, l: rate_v[pl.ds(g * 8, 8), pl.ds(l * 128, 128)])
    for m in range(MODES):
        rate = mode(m)
        rate_m[m] = rate
        dec1[m] = jnp.exp(rate * (-1.0 * LEN))
        pw[m] = jnp.exp(rate * -gap) * alive
        s = rate * (1.0 / RATE_HALF) - 1.0
        older, newer = jnp.ones_like(s), s
        tt[m, 0] = older
        tt[m, 1] = newer
        for k in range(2, ORD):
            older, newer = newer, 2.0 * s * newer - older
            tt[m, k] = newer

    for copy in consts[:2]:
        copy.wait()
    for c in range(6):
        if c % 2 == 0:
            xcopies[c // 2].wait()
        for n in range(4):
            z = dot(ends[...], x[pl.ds(c * LEN, LEN), pl.ds(n * 256, 256)])
            z = z[:ORD] + z[ORD:]
            for g in range(2):
                for h in range(2):
                    zrel[c, pl.ds(g * 64 + (2 * n + h) * 8, 8), :] = z[
                        g * 8 : g * 8 + 8, h * 128 : h * 128 + 128
                    ]

    for c in range(6):
        for k in range(ORD):
            zd[c, k] = zrel[c, pl.ds(k // 8 * 64 + k % 8, 8, stride=8), :]

    @pl.loop(0, MODES, step=4)
    def _(first):
        e = [[None] * 6 for _ in range(4)]
        for k in range(ORD):
            z = [zd[c, k] for c in range(6)]
            for i in range(4):
                t = tt[first + i, k]
                for c in range(6):
                    e[i][c] = t * z[c] if k == 0 else e[i][c] + t * z[c]
        for i in range(4):
            m = first + i
            d1 = dec1[m]
            mid[0, m] = e[i][2]
            mid[1, m] = e[i][4]
            past = (e[i][0] * d1 + e[i][1]) * pw[m]
            high = past.astype(BF16).astype(F32)
            send1[m, 0] = jnp.concatenate([high, past - high], 0).astype(BF16)
            own = [e[i][2] * d1 + e[i][3], e[i][4] * d1 + e[i][5]]
            send1[m, 1] = jnp.concatenate(own, 0).astype(BF16)

    pl.semaphore_wait(barrier, replies + CH - 1)

    for i, to in enumerate(SERVERS):
        part = send1.at[i]

        @pl.when(me != to)
        def _():
            pltpu.make_async_remote_copy(
                src_ref=part, dst_ref=recv1.at[me], send_sem=s1, recv_sem=r1,
                device_id=(to, mc), device_id_type=MESH,
            ).start()

        @pl.when(me == to)
        def _():
            recv1[me] = part[...]

    for copy in small[1:] + consts[2:] + [gate_copy]:
        copy.start()
    for copy in small[1:]:
        copy.wait()

    lane = lax.broadcasted_iota(jnp.int32, (8, 128), 1)

    def place(s, value):
        return jnp.where(lane == order[s], s, value)

    idx_v[...] = lax.fori_loop(0, 2 * CTX, place, jnp.zeros((8, 128), jnp.int32), unroll=8)
    idx_copy = pltpu.make_async_copy(idx_v, idx_s, sem_idx)
    idx_copy.start()

    spread(lambda g, l: res_v[pl.ds(g * 8, 8), pl.ds(l * 128, 128)])
    for m in range(MODES):
        rate = rate_m[m]
        step1[m] = jnp.exp(-rate)
        d2 = jnp.exp(rate * (-2.0 * LEN))
        dec2[m] = d2
        coef[m] = jnp.sqrt(2.0 * rate) * mode(m)

    for copy in consts[2:]:
        copy.wait()

    def natural(tiles, rows):
        for l in range(TILES):
            high, low = split(tiles[pl.ds(l, ORD, stride=8), :])
            rows[:, pl.ds(l * 128, 128)] = jnp.concatenate([high, high, low], 0)

    @pl.loop(0, ORD, step=4)
    def _(first):
        total = [None] * 4
        for m in range(MODES):
            for i in range(4):
                term = tt[m, first + i] * coef[m]
                total[i] = term if m == 0 else total[i] + term
        for i in range(4):
            grel[pl.ds(pl.multiple_of((first + i) * 8, 8), 8), :] = total[i]

    natural(grel, hb)

    @pl.loop(0, 4)
    def _(n):
        cols = pl.ds(pl.multiple_of(n * 256, 256), 256)
        both = dot(taps[:, : 3 * ORD], hb[:, cols])
        hr[:, cols] = both[:LEN]
        hi[:, cols] = both[LEN:]

    def near_chunk(c):
        rows = pl.ds(pl.multiple_of(c * LEN, LEN), LEN)
        xrows = pl.ds(pl.multiple_of((c + 2) * LEN, LEN), LEN)
        cols = [pl.ds(n * 256, 256) for n in range(4)]
        low, high = pl.ds(0, LEN), pl.ds(LEN, LEN)

        def to_spectrum(n):
            spec[n] = dot(forward[...], x[xrows, cols[n]])

        to_spectrum(0)
        for n in range(4):
            if n < 3:
                to_spectrum(n + 1)
            xr, xi = spec[n, low, :], spec[n, high, :]
            tr, ti = hr[:, cols[n]], hi[:, cols[n]]
            prod[n, low, :] = (xr * tr - xi * ti).astype(BF16)
            prod[n, high, :] = (xr * ti + xi * tr).astype(BF16)
            near[rows, cols[n]] = dot(inverse[...], prod[n])

    pl.loop(0, 2)(near_chunk)

    idx_copy.wait()

    @pl.when(serves)
    def _():
        first31 = recv1.at[pl.ds(0, CTX - 1)]
        pltpu.make_async_copy(first31, first31, r1).wait()
        parts = [None] * 4
        for c in range(CTX):
            past = recv1[c, 0].astype(F32)
            past = past[:8] + past[8:]
            parts[c % 4] = past if c < 4 else parts[c % 4] + past
            left = recv1[c, 1].astype(F32)
            ends_of[2 * c] = left[:8]
            ends_of[2 * c + 1] = left[8:]
        state = (parts[0] + parts[1]) + (parts[2] + parts[3])
        a = dec2[number]
        aa = a * a
        for j in range(CTX):
            first, second = [ends_of[idx_s[0, 2 * j + q]] for q in range(2)]
            incoming[2 * j] = state
            incoming[2 * j + 1] = a * state + first
            state = aa * state + (a * first + second)
        for c in range(CTX):
            both = [incoming[order[2 * c + q]] for q in range(2)]
            send2[c] = jnp.concatenate(both, 0).astype(BF16)
        for to in BY_START:

            @pl.when(me != to)
            def _():
                pltpu.make_async_remote_copy(
                    src_ref=send2.at[to], dst_ref=recv2.at[number],
                    send_sem=s2, recv_sem=r2, device_id=(to, mc), device_id_type=MESH,
                ).start()

        recv2[number] = send2[me]

    pl.loop(2, 4)(near_chunk)

    gate_copy.wait()
    @pl.when(serves)
    def _():
        rest = recv2.at[pl.ds(0, MODES - 1)]
        pltpu.make_async_copy(rest, rest, r2).wait()

    @pl.when(jnp.logical_not(serves))
    def _():
        pltpu.make_async_copy(recv2, recv2, r2).wait()


    for m in range(MODES):
        scale = coef[m] * step1[m]
        both = recv2[m].astype(F32)
        for q in range(2):
            state = both[8 * q : 8 * q + 8]
            gm[2 * q, m] = state * scale
            gm[2 * q + 1, m] = (state * dec1[m] + mid[q, m]) * scale

    @pl.loop(0, ORD, step=4)
    def _(first):
        g = [[None] * 4 for _ in range(4)]
        for m in range(MODES):
            u = [gm[c, m] for c in range(4)]
            for i in range(4):
                t = tt[m, first + i]
                for c in range(4):
                    g[i][c] = t * u[c] if m == 0 else g[i][c] + t * u[c]
        for i in range(4):
            for c in range(4):
                gb[c, pl.ds(pl.multiple_of((first + i) * 8, 8), 8), :] = g[i][c]

    for c in range(4):
        natural(gb.at[c], hf.at[c])

    ones = jnp.ones((8, 128), BF16)
    for c in range(4):
        rows = pl.ds(c * LEN, LEN)
        for n in range(4):
            cols = pl.ds(n * 256, 256)
            value = near[rows, cols] + dot(fart[:, : 3 * ORD], hf[c, :, cols])
            value = value * gt[rows, cols].astype(F32)
            near[rows, cols] = value
            square = value * value
            square = square[:, :128] + square[:, 128:]
            acc[c] = square if n == 0 else acc[c] + square
        high, low = split(acc[c])
        dims = (((1,), (1,)), ((), ()))
        sums = lax.dot_general(ones, high, dims, preferred_element_type=F32)
        sums = sums + lax.dot_general(ones, low, dims, preferred_element_type=F32)
        ss[c, pl.ds(0, 1), :] = sums[:1, :128]
        ss[c, pl.ds(1, 1), :] = sums[:1, 128:]
        for to in others:
            pltpu.make_async_remote_copy(
                src_ref=ss.at[c], dst_ref=rss.at[c, mc], send_sem=s3, recv_sem=r3.at[c],
                device_id=(me, to), device_id_type=MESH,
            ).start()
        rss[c, mc] = ss[c]

    for c in range(4):
        three = rss.at[c, pl.ds(0, CH - 1)]
        pltpu.make_async_copy(three, three, r3.at[c]).wait()
        total = (rss[c, 0] + rss[c, 1]) + (rss[c, 2] + rss[c, 3])
        factor = lax.rsqrt(total * (1.0 / (CH * CHANS)) + EPS)
        for g in range(2):
            rows = pl.ds(c * LEN + g * 128, 128)
            column = jnp.transpose(jnp.broadcast_to(factor[g : g + 1, :], (128, 128)))
            for l in range(TILES):
                cols = pl.ds(l * 128, 128)
                out[rows, cols] = (near[rows, cols] * column * gain_v[:, cols]).astype(BF16)

    @pl.when(jnp.logical_not(serves))
    def _():
        pltpu.make_async_copy(send1, send1, s1).wait()

    @pl.when(serves)
    def _():
        rest = send1.at[pl.ds(0, MODES - 1)]
        pltpu.make_async_copy(rest, rest, s1).wait()
        sent = send2.at[pl.ds(0, CTX - 1)]
        pltpu.make_async_copy(sent, sent, s2).wait()

    pltpu.make_async_copy(rss.at[pl.ds(0, CH - 1)], rss.at[pl.ds(0, CH - 1)], s3).wait()


def local(prefix, suffix, gates, rates, residues, gain, order, blocks):
    packed, places = tables()
    hbm = pl.BlockSpec(memory_space=pltpu.HBM)
    vmem = pltpu.VMEM
    dma = pltpu.SemaphoreType.DMA
    scratch = [
        pltpu.SMEM((2 * CTX,), jnp.int32),
        vmem((6 * LEN, CHANS), BF16),
        vmem((4 * LEN, CHANS), BF16),
        vmem((4 * LEN, CHANS), F32),
        vmem((MODES, CHANS), F32),
        vmem((MODES, CHANS), F32),
        vmem((1, CHANS), F32),
        vmem((2 * ORD, LEN), BF16),
        vmem((2 * LEN, LEN), BF16),
        vmem((LEN, 2 * LEN), BF16),
        vmem((2 * LEN, 128), BF16),
        vmem((LEN, 128), BF16),
        vmem((8, 128), jnp.int32),
        pltpu.SMEM((8, 128), jnp.int32),
        vmem((128, 128), F32),
        vmem((6, 128, 128), F32),
        vmem((6, ORD, 8, 128), F32),
        vmem((MODES, ORD, 8, 128), F32),
        vmem((MODES, 8, 128), F32),
        vmem((MODES, 8, 128), F32),
        vmem((MODES, 8, 128), F32),
        vmem((MODES, 8, 128), F32),
        vmem((MODES, 8, 128), F32),
        vmem((MODES, 8, 128), F32),
        vmem((2, MODES, 8, 128), F32),
        vmem((4, 2 * LEN, 256), F32),
        vmem((4, 2 * LEN, 256), BF16),
        vmem((LEN, CHANS), F32),
        vmem((LEN, CHANS), F32),
        vmem((3 * ORD, CHANS), BF16),
        vmem((128, 128), F32),
        vmem((4, MODES, 8, 128), F32),
        vmem((4, 128, 128), F32),
        vmem((4, 3 * ORD, CHANS), BF16),
        vmem((MODES, 2, 16, 128), BF16),
        vmem((CTX, 2, 16, 128), BF16),
        vmem((2 * CTX, 8, 128), F32),
        vmem((2 * CTX, 8, 128), F32),
        vmem((CTX, 16, 128), BF16),
        vmem((MODES, 16, 128), BF16),
        vmem((4, LEN, 128), F32),
        vmem((4, 2, 128), F32),
        vmem((4, CH, 2, 128), F32),
        dma((4,)),
        dma((3,)),
        dma,
        dma((len(places),)),
        dma,
        dma, dma, dma, dma, dma, dma((4,)),
    ]
    operands = (
        order, prefix, suffix, gates, rates, residues, gain[None, :], jnp.asarray(packed)
    )
    return pl.pallas_call(
        functools.partial(kernel, places),
        out_shape=pltpu.VMEM((4 * LEN, CHANS), BF16),
        in_specs=[pl.BlockSpec(memory_space=pltpu.SMEM)] + [hbm] * 8,
        out_specs=pl.BlockSpec(memory_space=pltpu.VMEM),
        scratch_shapes=scratch,
        compiler_params=pltpu.CompilerParams(
            collective_id=0, has_side_effects=True, vmem_limit_bytes=48 * 1024 * 1024
        ),
        cost_estimate=pl.CostEstimate(
            flops=6_000_000_000, bytes_accessed=8_000_000, transcendentals=100_000
        ),
    )(blocks, *(pltpu.with_memory_space_constraint(a, pltpu.HBM) for a in operands))


def solution(mesh):
    return jax.shard_map(
        local,
        mesh=mesh,
        in_specs=(
            P("ctx", "ch"),
            P("ctx", "ch"),
            P("ctx", "ch"),
            P(None, "ch"),
            P(None, "ch"),
            P("ch"),
            P(),
            P(),
        ),
        out_specs=P("ctx", "ch"),
        check_vma=False,
    )
```

```python
import functools

import jax
import jax.numpy as jnp
import ml_dtypes
import numpy as np
from jax import lax
from jax.experimental import pallas as pl
from jax.experimental.pallas import tpu as pltpu
from jax.sharding import PartitionSpec as P

MESH = pl.DeviceIdType.MESH
F32 = jnp.float32
BF16 = jnp.bfloat16

LEN = 256
ORD = 16
MODES = 16
CTX = 32
CH = 4
CHANS = 1024
TILES = CHANS // 128
RATE_HALF = 1.0 / 48.0
EPS = 1e-6


def series():
    nodes = 64
    angle = np.pi * (np.arange(nodes) + 0.5) / nodes
    rate = RATE_HALF * (1.0 + np.cos(angle))
    values = np.exp(-rate[:, None] * np.arange(LEN)[None, :])
    basis = np.cos(np.arange(ORD)[:, None] * angle[None, :])
    psi = 2.0 / nodes * (basis @ values)
    psi[0] *= 0.5
    return psi


def halves(a):
    high = a.astype(np.float32).astype(ml_dtypes.bfloat16)
    low = (a - high.astype(np.float64)).astype(np.float32).astype(ml_dtypes.bfloat16)
    return high, low


def tables():
    psi = series()
    theta = np.pi / (2 * LEN) * np.outer(2 * np.arange(LEN) + 1, np.arange(LEN))
    forward = np.concatenate([np.cos(theta), -np.sin(theta)], 0)
    inverse = np.concatenate([np.cos(theta).T, -np.sin(theta).T], 1) / LEN
    to_bf16 = lambda a: a.astype(np.float32).astype(ml_dtypes.bfloat16)
    ends = np.concatenate(halves(psi[:, ::-1]), 0)
    th, tl = halves(forward @ psi.T)
    fh, fl = halves(psi.T)
    arrays = (
        ends,
        np.concatenate([th, tl, th], 1),
        to_bf16(forward),
        to_bf16(inverse),
        np.concatenate([fh, fl, fh], 1),
    )
    slabs, places, row = [], [], 0
    for a in arrays:
        a = np.pad(a, ((0, 0), (0, -a.shape[1] % 128)))
        for col in range(0, a.shape[1], 128):
            slabs.append(a[:, col : col + 128])
            places.append((row, a.shape[0], col))
            row += a.shape[0]
    return np.concatenate(slabs, 0), places


def place_of(ctx):
    return ctx // 16, ctx // 4 % 4, ctx % 4


def lateness(ctx):
    x, z, y = place_of(ctx)
    return 1.5 * x + 1.0 * z + 0.85 * y


BY_START = sorted(range(CTX), key=lateness)
SERVERS = BY_START[:8]
PER = MODES // len(SERVERS)


def split(a):
    high = a.astype(BF16)
    low = (a - high.astype(F32)).astype(BF16)
    return high, low


def dot(a, b):
    return jnp.dot(a, b, preferred_element_type=F32)


def kernel(
    places,
    blocks, order_h, prefix, suffix, gates, rates, residues, gain, packed,
    out,
    order, x, gt, near, rate_v, res_v, gain_v,
    ends, forward, inverse, taps, fart,
    idx_v, idx_s,
    relay, zrel, zd, tt, rate_m, coef, step1, dec1, dec2, pw,
    mid, spec, prod, hr, hi, hb, grel, gm, gb, hf,
    send1, recv1, incoming, send2, recv2, acc, ss, rss,
    sem_small, sem_x, sem_gate, sem_const, sem_idx,
    s1, r1, s2, r2, s3, r3,
):
    me = lax.axis_index("ctx")
    mc = lax.axis_index("ch")

    small = [
        pltpu.make_async_copy(rates, rate_v, sem_small.at[0]),
        pltpu.make_async_copy(residues, res_v, sem_small.at[1]),
        pltpu.make_async_copy(order_h, order, sem_small.at[2]),
        pltpu.make_async_copy(gain, gain_v, sem_small.at[3]),
    ]
    targets = [ends] * 2 + [taps] + [forward] * 2 + [inverse] * 4 + [fart]
    consts = [
        pltpu.make_async_copy(
            packed.at[pl.ds(row, count)], target.at[:, pl.ds(col, 128)], sem_const.at[i]
        )
        for i, ((row, count, col), target) in enumerate(zip(places, targets))
    ]
    xcopies = [
        pltpu.make_async_copy(prefix, x.at[pl.ds(0, 2 * LEN)], sem_x.at[0]),
        pltpu.make_async_copy(
            suffix.at[pl.ds(0, 2 * LEN)], x.at[pl.ds(2 * LEN, 2 * LEN)], sem_x.at[1]
        ),
        pltpu.make_async_copy(
            suffix.at[pl.ds(2 * LEN, 2 * LEN)], x.at[pl.ds(4 * LEN, 2 * LEN)], sem_x.at[2]
        ),
    ]
    gate_copy = pltpu.make_async_copy(gates, gt, sem_gate)
    for copy in small[:1] + consts[:2] + xcopies:
        copy.start()

    barrier = pltpu.get_barrier_semaphore()
    others = [lax.rem(mc + r, CH) for r in (2, 3, 1)]
    serves = functools.reduce(jnp.logical_or, [me == ctx for ctx in SERVERS])
    number = sum(jnp.where(me == ctx, i, 0) for i, ctx in enumerate(SERVERS))
    replies = len(SERVERS) - jnp.where(serves, 1, 0)

    @pl.when(serves)
    def _():
        for to in BY_START:

            @pl.when(me != to)
            def _():
                pl.semaphore_signal(barrier, inc=1, device_id=(to, mc), device_id_type=MESH)

    for to in others:
        pl.semaphore_signal(barrier, inc=1, device_id=(me, to), device_id_type=MESH)

    small[0].wait()

    def spread(read):
        for g in range(2):
            for l in range(TILES):
                relay[pl.ds(g * 64 + l * 8, 8), :] = read(g, l)

    def mode(m):
        return relay[pl.ds(m // 8 * 64 + m % 8, 8, stride=8), :]

    live = blocks[0]
    gap = jnp.maximum(live - 1 - me, 0).astype(F32) * (2.0 * LEN)
    alive = jnp.where(me < live, 1.0, 0.0).astype(F32)
    spread(lambda g, l: rate_v[pl.ds(g * 8, 8), pl.ds(l * 128, 128)])
    for m in range(MODES):
        rate = mode(m)
        rate_m[m] = rate
        dec1[m] = jnp.exp(rate * (-1.0 * LEN))
        pw[m] = jnp.exp(rate * -gap) * alive
        s = rate * (1.0 / RATE_HALF) - 1.0
        older, newer = jnp.ones_like(s), s
        tt[m, 0] = older
        tt[m, 1] = newer
        for k in range(2, ORD):
            older, newer = newer, 2.0 * s * newer - older
            tt[m, k] = newer

    for copy in consts[:2]:
        copy.wait()
    for c in range(6):
        if c % 2 == 0:
            xcopies[c // 2].wait()
        for n in range(4):
            z = dot(ends[...], x[pl.ds(c * LEN, LEN), pl.ds(n * 256, 256)])
            z = z[:ORD] + z[ORD:]
            for g in range(2):
                for h in range(2):
                    zrel[c, pl.ds(g * 64 + (2 * n + h) * 8, 8), :] = z[
                        g * 8 : g * 8 + 8, h * 128 : h * 128 + 128
                    ]

    for c in range(6):
        for k in range(ORD):
            zd[c, k] = zrel[c, pl.ds(k // 8 * 64 + k % 8, 8, stride=8), :]

    @pl.loop(0, MODES, step=4)
    def _(first):
        e = [[None] * 6 for _ in range(4)]
        for k in range(ORD):
            z = [zd[c, k] for c in range(6)]
            for i in range(4):
                t = tt[first + i, k]
                for c in range(6):
                    e[i][c] = t * z[c] if k == 0 else e[i][c] + t * z[c]
        for j in range(2):
            states = [[], [], []]
            for i in (2 * j, 2 * j + 1):
                m = first + i
                d1 = dec1[m]
                mid[0, m] = e[i][2]
                mid[1, m] = e[i][4]
                states[0].append((e[i][0] * d1 + e[i][1]) * pw[m])
                states[1].append(e[i][2] * d1 + e[i][3])
                states[2].append(e[i][4] * d1 + e[i][5])
            for q in range(3):
                send1[first // 2 + j, q] = jnp.concatenate(states[q], 0).astype(BF16)

    pl.semaphore_wait(barrier, replies + CH - 1)

    for i, to in enumerate(SERVERS):
        part = send1.at[i]

        @pl.when(me != to)
        def _():
            pltpu.make_async_remote_copy(
                src_ref=part, dst_ref=recv1.at[me], send_sem=s1, recv_sem=r1,
                device_id=(to, mc), device_id_type=MESH,
            ).start()

        @pl.when(me == to)
        def _():
            recv1[me] = part[...]

    for copy in small[1:] + consts[2:] + [gate_copy]:
        copy.start()
    for copy in small[1:]:
        copy.wait()

    lane = lax.broadcasted_iota(jnp.int32, (8, 128), 1)

    def place(s, value):
        return jnp.where(lane == order[s], s, value)

    idx_v[...] = lax.fori_loop(0, 2 * CTX, place, jnp.zeros((8, 128), jnp.int32), unroll=8)
    idx_copy = pltpu.make_async_copy(idx_v, idx_s, sem_idx)
    idx_copy.start()

    spread(lambda g, l: res_v[pl.ds(g * 8, 8), pl.ds(l * 128, 128)])
    for m in range(MODES):
        rate = rate_m[m]
        step1[m] = jnp.exp(-rate)
        d2 = jnp.exp(rate * (-2.0 * LEN))
        dec2[m] = d2
        coef[m] = jnp.sqrt(2.0 * rate) * mode(m)

    for copy in consts[2:]:
        copy.wait()

    def natural(tiles, rows):
        for l in range(TILES):
            high, low = split(tiles[pl.ds(l, ORD, stride=8), :])
            rows[:, pl.ds(l * 128, 128)] = jnp.concatenate([high, high, low], 0)

    @pl.loop(0, ORD, step=4)
    def _(first):
        total = [None] * 4
        for m in range(MODES):
            for i in range(4):
                term = tt[m, first + i] * coef[m]
                total[i] = term if m == 0 else total[i] + term
        for i in range(4):
            grel[pl.ds(pl.multiple_of((first + i) * 8, 8), 8), :] = total[i]

    natural(grel, hb)

    @pl.loop(0, 4)
    def _(n):
        cols = pl.ds(pl.multiple_of(n * 256, 256), 256)
        both = dot(taps[:, : 3 * ORD], hb[:, cols])
        hr[:, cols] = both[:LEN]
        hi[:, cols] = both[LEN:]

    def near_chunk(c):
        rows = pl.ds(pl.multiple_of(c * LEN, LEN), LEN)
        xrows = pl.ds(pl.multiple_of((c + 2) * LEN, LEN), LEN)
        cols = [pl.ds(n * 256, 256) for n in range(4)]
        low, high = pl.ds(0, LEN), pl.ds(LEN, LEN)

        def to_spectrum(n):
            spec[n] = dot(forward[...], x[xrows, cols[n]])

        to_spectrum(0)
        for n in range(4):
            if n < 3:
                to_spectrum(n + 1)
            xr, xi = spec[n, low, :], spec[n, high, :]
            tr, ti = hr[:, cols[n]], hi[:, cols[n]]
            prod[n, low, :] = (xr * tr - xi * ti).astype(BF16)
            prod[n, high, :] = (xr * ti + xi * tr).astype(BF16)
            near[rows, cols[n]] = dot(inverse[...], prod[n])

    pl.loop(0, 2)(near_chunk)

    idx_copy.wait()

    @pl.when(serves)
    def _():
        first31 = recv1.at[pl.ds(0, CTX - 1)]
        pltpu.make_async_copy(first31, first31, r1).wait()
        parts = [None] * 4
        for c in range(CTX):
            past = recv1[c, 0].astype(F32)
            parts[c % 4] = past if c < 4 else parts[c % 4] + past
        state = (parts[0] + parts[1]) + (parts[2] + parts[3])
        a = jnp.concatenate([dec2[PER * number + i] for i in range(PER)], 0)
        aa = a * a
        for j in range(CTX):
            slots = [idx_s[0, 2 * j + q] for q in range(2)]
            first, second = [
                recv1[lax.div(slot, 2), 1 + lax.rem(slot, 2)].astype(F32) for slot in slots
            ]
            incoming[2 * j] = state
            incoming[2 * j + 1] = a * state + first
            state = aa * state + (a * first + second)
        for c in range(CTX):
            for q in range(2):
                send2[c, q] = incoming[order[2 * c + q]].astype(BF16)
        for to in BY_START:

            @pl.when(me != to)
            def _():
                pltpu.make_async_remote_copy(
                    src_ref=send2.at[to], dst_ref=recv2.at[number],
                    send_sem=s2, recv_sem=r2, device_id=(to, mc), device_id_type=MESH,
                ).start()

        recv2[number] = send2[me]

    pl.loop(2, 4)(near_chunk)

    gate_copy.wait()
    @pl.when(serves)
    def _():
        rest = recv2.at[pl.ds(0, len(SERVERS) - 1)]
        pltpu.make_async_copy(rest, rest, r2).wait()

    @pl.when(jnp.logical_not(serves))
    def _():
        pltpu.make_async_copy(recv2, recv2, r2).wait()


    for i in range(len(SERVERS)):
        for q in range(2):
            both = recv2[i, q].astype(F32)
            for j in range(PER):
                m = PER * i + j
                state = both[8 * j : 8 * j + 8]
                scale = coef[m] * step1[m]
                gm[2 * q, m] = state * scale
                gm[2 * q + 1, m] = (state * dec1[m] + mid[q, m]) * scale

    @pl.loop(0, ORD, step=4)
    def _(first):
        g = [[None] * 4 for _ in range(4)]
        for m in range(MODES):
            u = [gm[c, m] for c in range(4)]
            for i in range(4):
                t = tt[m, first + i]
                for c in range(4):
                    g[i][c] = t * u[c] if m == 0 else g[i][c] + t * u[c]
        for i in range(4):
            for c in range(4):
                gb[c, pl.ds(pl.multiple_of((first + i) * 8, 8), 8), :] = g[i][c]

    for c in range(4):
        natural(gb.at[c], hf.at[c])

    ones = jnp.ones((8, 128), BF16)
    for c in range(4):
        rows = pl.ds(c * LEN, LEN)
        for n in range(4):
            cols = pl.ds(n * 256, 256)
            value = near[rows, cols] + dot(fart[:, : 3 * ORD], hf[c, :, cols])
            value = value * gt[rows, cols].astype(F32)
            near[rows, cols] = value
            square = value * value
            square = square[:, :128] + square[:, 128:]
            acc[c] = square if n == 0 else acc[c] + square
        high, low = split(acc[c])
        dims = (((1,), (1,)), ((), ()))
        sums = lax.dot_general(ones, high, dims, preferred_element_type=F32)
        sums = sums + lax.dot_general(ones, low, dims, preferred_element_type=F32)
        ss[c, pl.ds(0, 1), :] = sums[:1, :128]
        ss[c, pl.ds(1, 1), :] = sums[:1, 128:]
        for to in others:
            pltpu.make_async_remote_copy(
                src_ref=ss.at[c], dst_ref=rss.at[c, mc], send_sem=s3, recv_sem=r3.at[c],
                device_id=(me, to), device_id_type=MESH,
            ).start()
        rss[c, mc] = ss[c]

    for c in range(4):
        three = rss.at[c, pl.ds(0, CH - 1)]
        pltpu.make_async_copy(three, three, r3.at[c]).wait()
        total = (rss[c, 0] + rss[c, 1]) + (rss[c, 2] + rss[c, 3])
        factor = lax.rsqrt(total * (1.0 / (CH * CHANS)) + EPS)
        for g in range(2):
            rows = pl.ds(c * LEN + g * 128, 128)
            column = jnp.transpose(jnp.broadcast_to(factor[g : g + 1, :], (128, 128)))
            for l in range(TILES):
                cols = pl.ds(l * 128, 128)
                out[rows, cols] = (near[rows, cols] * column * gain_v[:, cols]).astype(BF16)

    @pl.when(jnp.logical_not(serves))
    def _():
        pltpu.make_async_copy(send1, send1, s1).wait()

    @pl.when(serves)
    def _():
        rest = send1.at[pl.ds(0, len(SERVERS) - 1)]
        pltpu.make_async_copy(rest, rest, s1).wait()
        sent = send2.at[pl.ds(0, CTX - 1)]
        pltpu.make_async_copy(sent, sent, s2).wait()

    pltpu.make_async_copy(rss.at[pl.ds(0, CH - 1)], rss.at[pl.ds(0, CH - 1)], s3).wait()


def local(prefix, suffix, gates, rates, residues, gain, order, blocks):
    packed, places = tables()
    hbm = pl.BlockSpec(memory_space=pltpu.HBM)
    vmem = pltpu.VMEM
    dma = pltpu.SemaphoreType.DMA
    scratch = [
        pltpu.SMEM((2 * CTX,), jnp.int32),
        vmem((6 * LEN, CHANS), BF16),
        vmem((4 * LEN, CHANS), BF16),
        vmem((4 * LEN, CHANS), F32),
        vmem((MODES, CHANS), F32),
        vmem((MODES, CHANS), F32),
        vmem((1, CHANS), F32),
        vmem((2 * ORD, LEN), BF16),
        vmem((2 * LEN, LEN), BF16),
        vmem((LEN, 2 * LEN), BF16),
        vmem((2 * LEN, 128), BF16),
        vmem((LEN, 128), BF16),
        vmem((8, 128), jnp.int32),
        pltpu.SMEM((8, 128), jnp.int32),
        vmem((128, 128), F32),
        vmem((6, 128, 128), F32),
        vmem((6, ORD, 8, 128), F32),
        vmem((MODES, ORD, 8, 128), F32),
        vmem((MODES, 8, 128), F32),
        vmem((MODES, 8, 128), F32),
        vmem((MODES, 8, 128), F32),
        vmem((MODES, 8, 128), F32),
        vmem((MODES, 8, 128), F32),
        vmem((MODES, 8, 128), F32),
        vmem((2, MODES, 8, 128), F32),
        vmem((4, 2 * LEN, 256), F32),
        vmem((4, 2 * LEN, 256), BF16),
        vmem((LEN, CHANS), F32),
        vmem((LEN, CHANS), F32),
        vmem((3 * ORD, CHANS), BF16),
        vmem((128, 128), F32),
        vmem((4, MODES, 8, 128), F32),
        vmem((4, 128, 128), F32),
        vmem((4, 3 * ORD, CHANS), BF16),
        vmem((len(SERVERS), 3, 16, 128), BF16),
        vmem((CTX, 3, 16, 128), BF16),
        vmem((2 * CTX, 16, 128), F32),
        vmem((CTX, 2, 16, 128), BF16),
        vmem((len(SERVERS), 2, 16, 128), BF16),
        vmem((4, LEN, 128), F32),
        vmem((4, 2, 128), F32),
        vmem((4, CH, 2, 128), F32),
        dma((4,)),
        dma((3,)),
        dma,
        dma((len(places),)),
        dma,
        dma, dma, dma, dma, dma, dma((4,)),
    ]
    operands = (
        order, prefix, suffix, gates, rates, residues, gain[None, :], jnp.asarray(packed)
    )
    return pl.pallas_call(
        functools.partial(kernel, places),
        out_shape=pltpu.VMEM((4 * LEN, CHANS), BF16),
        in_specs=[pl.BlockSpec(memory_space=pltpu.SMEM)] + [hbm] * 8,
        out_specs=pl.BlockSpec(memory_space=pltpu.VMEM),
        scratch_shapes=scratch,
        compiler_params=pltpu.CompilerParams(
            collective_id=0, has_side_effects=True, vmem_limit_bytes=48 * 1024 * 1024
        ),
        cost_estimate=pl.CostEstimate(
            flops=6_000_000_000, bytes_accessed=8_000_000, transcendentals=100_000
        ),
    )(blocks, *(pltpu.with_memory_space_constraint(a, pltpu.HBM) for a in operands))


def solution(mesh):
    return jax.shard_map(
        local,
        mesh=mesh,
        in_specs=(
            P("ctx", "ch"),
            P("ctx", "ch"),
            P("ctx", "ch"),
            P(None, "ch"),
            P(None, "ch"),
            P("ch"),
            P(),
            P(),
        ),
        out_specs=P("ctx", "ch"),
        check_vma=False,
    )
```

```python
import functools

import jax
import jax.numpy as jnp
import ml_dtypes
import numpy as np
from jax import lax
from jax.experimental import pallas as pl
from jax.experimental.pallas import tpu as pltpu
from jax.sharding import PartitionSpec as P

MESH = pl.DeviceIdType.MESH
F32 = jnp.float32
BF16 = jnp.bfloat16

LEN = 256
ORD = 16
MODES = 16
CTX = 32
CH = 4
CHANS = 1024
TILES = CHANS // 128
RATE_HALF = 1.0 / 48.0
EPS = 1e-6


def series():
    nodes = 64
    angle = np.pi * (np.arange(nodes) + 0.5) / nodes
    rate = RATE_HALF * (1.0 + np.cos(angle))
    values = np.exp(-rate[:, None] * np.arange(LEN)[None, :])
    basis = np.cos(np.arange(ORD)[:, None] * angle[None, :])
    psi = 2.0 / nodes * (basis @ values)
    psi[0] *= 0.5
    return psi


def halves(a):
    high = a.astype(np.float32).astype(ml_dtypes.bfloat16)
    low = (a - high.astype(np.float64)).astype(np.float32).astype(ml_dtypes.bfloat16)
    return high, low


def tables():
    psi = series()
    theta = np.pi / (2 * LEN) * np.outer(2 * np.arange(LEN) + 1, np.arange(LEN))
    forward = np.concatenate([np.cos(theta), -np.sin(theta)], 0)
    inverse = np.concatenate([np.cos(theta).T, -np.sin(theta).T], 1) / LEN
    to_bf16 = lambda a: a.astype(np.float32).astype(ml_dtypes.bfloat16)
    ends = np.concatenate(halves(psi[:, ::-1]), 0)
    th, tl = halves(forward @ psi.T)
    fh, fl = halves(psi.T)
    arrays = (
        ends,
        np.concatenate([th, tl, th], 1),
        to_bf16(forward),
        to_bf16(inverse),
        np.concatenate([fh, fl, fh], 1),
    )
    slabs, places, row = [], [], 0
    for a in arrays:
        a = np.pad(a, ((0, 0), (0, -a.shape[1] % 128)))
        for col in range(0, a.shape[1], 128):
            slabs.append(a[:, col : col + 128])
            places.append((row, a.shape[0], col))
            row += a.shape[0]
    return np.concatenate(slabs, 0), places


def place_of(ctx):
    return ctx // 16, ctx // 4 % 4, ctx % 4


def lateness(ctx):
    x, z, y = place_of(ctx)
    return 1.5 * x + 1.0 * z + 0.85 * y


BY_START = sorted(range(CTX), key=lateness)
SERVERS = [0, 1, 4, 16, 2, 8, 3, 20]
PER = MODES // len(SERVERS)


def split(a):
    high = a.astype(BF16)
    low = (a - high.astype(F32)).astype(BF16)
    return high, low


def dot(a, b):
    return jnp.dot(a, b, preferred_element_type=F32)


def kernel(
    places,
    blocks, order_h, prefix, suffix, gates, rates, residues, gain, packed,
    out,
    order, x, gt, near, rate_v, res_v, gain_v,
    ends, forward, inverse, taps, fart,
    idx_v, idx_s,
    relay, zrel, zd, tt, rate_m, coef, step1, dec1, dec2, pw,
    mid, spec, prod, hr, hi, hb, grel, gm, gb, hf,
    send1, recv1, incoming, send2, recv2, acc, ss, rss,
    sem_small, sem_x, sem_gate, sem_const, sem_idx,
    s1, r1, s2, r2, s3, r3,
):
    me = lax.axis_index("ctx")
    mc = lax.axis_index("ch")

    small = [
        pltpu.make_async_copy(rates, rate_v, sem_small.at[0]),
        pltpu.make_async_copy(residues, res_v, sem_small.at[1]),
        pltpu.make_async_copy(order_h, order, sem_small.at[2]),
        pltpu.make_async_copy(gain, gain_v, sem_small.at[3]),
    ]
    targets = [ends] * 2 + [taps] + [forward] * 2 + [inverse] * 4 + [fart]
    consts = [
        pltpu.make_async_copy(
            packed.at[pl.ds(row, count)], target.at[:, pl.ds(col, 128)], sem_const.at[i]
        )
        for i, ((row, count, col), target) in enumerate(zip(places, targets))
    ]
    xcopies = [
        pltpu.make_async_copy(prefix, x.at[pl.ds(0, 2 * LEN)], sem_x.at[0]),
        pltpu.make_async_copy(
            suffix.at[pl.ds(0, 2 * LEN)], x.at[pl.ds(2 * LEN, 2 * LEN)], sem_x.at[1]
        ),
        pltpu.make_async_copy(
            suffix.at[pl.ds(2 * LEN, 2 * LEN)], x.at[pl.ds(4 * LEN, 2 * LEN)], sem_x.at[2]
        ),
    ]
    gate_copy = pltpu.make_async_copy(gates, gt, sem_gate)
    for copy in small[:1] + consts[:2] + xcopies:
        copy.start()

    barrier = pltpu.get_barrier_semaphore()
    others = [lax.rem(mc + r, CH) for r in (2, 3, 1)]
    serves = functools.reduce(jnp.logical_or, [me == ctx for ctx in SERVERS])
    number = sum(jnp.where(me == ctx, i, 0) for i, ctx in enumerate(SERVERS))
    replies = len(SERVERS) - jnp.where(serves, 1, 0)

    @pl.when(serves)
    def _():
        for to in BY_START:

            @pl.when(me != to)
            def _():
                pl.semaphore_signal(barrier, inc=1, device_id=(to, mc), device_id_type=MESH)

    for to in others:
        pl.semaphore_signal(barrier, inc=1, device_id=(me, to), device_id_type=MESH)

    small[0].wait()

    def spread(read):
        for g in range(2):
            for l in range(TILES):
                relay[pl.ds(g * 64 + l * 8, 8), :] = read(g, l)

    def mode(m):
        return relay[pl.ds(m // 8 * 64 + m % 8, 8, stride=8), :]

    live = blocks[0]
    gap = jnp.maximum(live - 1 - me, 0).astype(F32) * (2.0 * LEN)
    alive = jnp.where(me < live, 1.0, 0.0).astype(F32)
    spread(lambda g, l: rate_v[pl.ds(g * 8, 8), pl.ds(l * 128, 128)])
    for m in range(MODES):
        rate = mode(m)
        rate_m[m] = rate
        dec1[m] = jnp.exp(rate * (-1.0 * LEN))
        pw[m] = jnp.exp(rate * -gap) * alive
        s = rate * (1.0 / RATE_HALF) - 1.0
        older, newer = jnp.ones_like(s), s
        tt[m, 0] = older
        tt[m, 1] = newer
        for k in range(2, ORD):
            older, newer = newer, 2.0 * s * newer - older
            tt[m, k] = newer

    for copy in consts[:2]:
        copy.wait()
    for c in range(6):
        if c % 2 == 0:
            xcopies[c // 2].wait()
        for n in range(4):
            z = dot(ends[...], x[pl.ds(c * LEN, LEN), pl.ds(n * 256, 256)])
            z = z[:ORD] + z[ORD:]
            for g in range(2):
                for h in range(2):
                    zrel[c, pl.ds(g * 64 + (2 * n + h) * 8, 8), :] = z[
                        g * 8 : g * 8 + 8, h * 128 : h * 128 + 128
                    ]
        for k in range(ORD):
            zd[c, k] = zrel[c, pl.ds(k // 8 * 64 + k % 8, 8, stride=8), :]

    @pl.loop(0, MODES, step=4)
    def _(first):
        e = [[None] * 6 for _ in range(4)]
        for k in range(ORD):
            z = [zd[c, k] for c in range(6)]
            for i in range(4):
                t = tt[first + i, k]
                for c in range(6):
                    e[i][c] = t * z[c] if k == 0 else e[i][c] + t * z[c]
        for j in range(2):
            states = [[], [], []]
            for i in (2 * j, 2 * j + 1):
                m = first + i
                d1 = dec1[m]
                mid[0, m] = e[i][2]
                mid[1, m] = e[i][4]
                states[0].append((e[i][0] * d1 + e[i][1]) * pw[m])
                states[1].append(e[i][2] * d1 + e[i][3])
                states[2].append(e[i][4] * d1 + e[i][5])
            for q in range(3):
                send1[first // 2 + j, q] = jnp.concatenate(states[q], 0).astype(BF16)

    pl.semaphore_wait(barrier, replies + CH - 1)

    for i, to in enumerate(SERVERS):
        part = send1.at[i]

        @pl.when(me != to)
        def _():
            pltpu.make_async_remote_copy(
                src_ref=part, dst_ref=recv1.at[me], send_sem=s1, recv_sem=r1,
                device_id=(to, mc), device_id_type=MESH,
            ).start()

        @pl.when(me == to)
        def _():
            recv1[me] = part[...]

    for copy in small[1:] + consts[2:] + [gate_copy]:
        copy.start()
    for copy in small[1:]:
        copy.wait()

    lane = lax.broadcasted_iota(jnp.int32, (8, 128), 1)

    def place(s, value):
        return jnp.where(lane == order[s], s, value)

    idx_v[...] = lax.fori_loop(0, 2 * CTX, place, jnp.zeros((8, 128), jnp.int32), unroll=8)
    idx_copy = pltpu.make_async_copy(idx_v, idx_s, sem_idx)
    idx_copy.start()

    spread(lambda g, l: res_v[pl.ds(g * 8, 8), pl.ds(l * 128, 128)])
    for m in range(MODES):
        rate = rate_m[m]
        step1[m] = jnp.exp(-rate)
        d2 = jnp.exp(rate * (-2.0 * LEN))
        dec2[m] = d2
        coef[m] = jnp.sqrt(2.0 * rate) * mode(m)

    for copy in consts[2:]:
        copy.wait()

    def natural(tiles, rows):
        for l in range(TILES):
            high, low = split(tiles[pl.ds(l, ORD, stride=8), :])
            rows[:, pl.ds(l * 128, 128)] = jnp.concatenate([high, high, low], 0)

    @pl.loop(0, ORD, step=4)
    def _(first):
        total = [None] * 4
        for m in range(MODES):
            for i in range(4):
                term = tt[m, first + i] * coef[m]
                total[i] = term if m == 0 else total[i] + term
        for i in range(4):
            grel[pl.ds(pl.multiple_of((first + i) * 8, 8), 8), :] = total[i]

    natural(grel, hb)

    @pl.loop(0, 4)
    def _(n):
        cols = pl.ds(pl.multiple_of(n * 256, 256), 256)
        both = dot(taps[:, : 3 * ORD], hb[:, cols])
        hr[:, cols] = both[:LEN]
        hi[:, cols] = both[LEN:]

    def near_chunk(c):
        rows = pl.ds(pl.multiple_of(c * LEN, LEN), LEN)
        xrows = pl.ds(pl.multiple_of((c + 2) * LEN, LEN), LEN)
        cols = [pl.ds(n * 256, 256) for n in range(4)]
        low, high = pl.ds(0, LEN), pl.ds(LEN, LEN)

        def to_spectrum(n):
            spec[n] = dot(forward[...], x[xrows, cols[n]])

        to_spectrum(0)
        for n in range(4):
            if n < 3:
                to_spectrum(n + 1)
            xr, xi = spec[n, low, :], spec[n, high, :]
            tr, ti = hr[:, cols[n]], hi[:, cols[n]]
            prod[n, low, :] = (xr * tr - xi * ti).astype(BF16)
            prod[n, high, :] = (xr * ti + xi * tr).astype(BF16)
            near[rows, cols[n]] = dot(inverse[...], prod[n])

    pl.loop(0, 2)(near_chunk)

    idx_copy.wait()

    @pl.when(serves)
    def _():
        first31 = recv1.at[pl.ds(0, CTX - 1)]
        pltpu.make_async_copy(first31, first31, r1).wait()
        parts = [None] * 4
        for c in range(CTX):
            past = recv1[c, 0].astype(F32)
            parts[c % 4] = past if c < 4 else parts[c % 4] + past
        state = (parts[0] + parts[1]) + (parts[2] + parts[3])
        a = jnp.concatenate([dec2[PER * number + i] for i in range(PER)], 0)
        aa = a * a
        for j in range(CTX):
            slots = [idx_s[0, 2 * j + q] for q in range(2)]
            first, second = [
                recv1[lax.div(slot, 2), 1 + lax.rem(slot, 2)].astype(F32) for slot in slots
            ]
            incoming[2 * j] = state
            incoming[2 * j + 1] = a * state + first
            state = aa * state + (a * first + second)
        for c in range(CTX):
            for q in range(2):
                send2[c, q] = incoming[order[2 * c + q]].astype(BF16)
        for to in BY_START:

            @pl.when(me != to)
            def _():
                pltpu.make_async_remote_copy(
                    src_ref=send2.at[to], dst_ref=recv2.at[number],
                    send_sem=s2, recv_sem=r2, device_id=(to, mc), device_id_type=MESH,
                ).start()

        recv2[number] = send2[me]

    pl.loop(2, 4)(near_chunk)

    gate_copy.wait()
    @pl.when(serves)
    def _():
        rest = recv2.at[pl.ds(0, len(SERVERS) - 1)]
        pltpu.make_async_copy(rest, rest, r2).wait()

    @pl.when(jnp.logical_not(serves))
    def _():
        pltpu.make_async_copy(recv2, recv2, r2).wait()


    for i in range(len(SERVERS)):
        for q in range(2):
            both = recv2[i, q].astype(F32)
            for j in range(PER):
                m = PER * i + j
                state = both[8 * j : 8 * j + 8]
                scale = coef[m] * step1[m]
                gm[2 * q, m] = state * scale
                gm[2 * q + 1, m] = (state * dec1[m] + mid[q, m]) * scale

    @pl.loop(0, ORD, step=4)
    def _(first):
        g = [[None] * 4 for _ in range(4)]
        for m in range(MODES):
            u = [gm[c, m] for c in range(4)]
            for i in range(4):
                t = tt[m, first + i]
                for c in range(4):
                    g[i][c] = t * u[c] if m == 0 else g[i][c] + t * u[c]
        for i in range(4):
            for c in range(4):
                gb[c, pl.ds(pl.multiple_of((first + i) * 8, 8), 8), :] = g[i][c]

    for c in range(4):
        natural(gb.at[c], hf.at[c])

    ones = jnp.ones((8, 128), BF16)
    for c in range(4):
        rows = pl.ds(c * LEN, LEN)
        for n in range(4):
            cols = pl.ds(n * 256, 256)
            value = near[rows, cols] + dot(fart[:, : 3 * ORD], hf[c, :, cols])
            value = value * gt[rows, cols].astype(F32)
            near[rows, cols] = value
            square = value * value
            square = square[:, :128] + square[:, 128:]
            acc[c] = square if n == 0 else acc[c] + square
        high, low = split(acc[c])
        dims = (((1,), (1,)), ((), ()))
        sums = lax.dot_general(ones, high, dims, preferred_element_type=F32)
        sums = sums + lax.dot_general(ones, low, dims, preferred_element_type=F32)
        ss[c, pl.ds(0, 1), :] = sums[:1, :128]
        ss[c, pl.ds(1, 1), :] = sums[:1, 128:]
        rss[c // 2, mc, c % 2] = ss[c]
        for to in others if c % 2 else []:
            pltpu.make_async_remote_copy(
                src_ref=ss.at[pl.ds(c - 1, 2)], dst_ref=rss.at[c // 2, mc], send_sem=s3, recv_sem=r3.at[c],
                device_id=(me, to), device_id_type=MESH,
            ).start()

    for c in range(4):
        if c % 2 == 0:
            three = rss.at[c // 2, pl.ds(0, CH - 1)]
            pltpu.make_async_copy(three, three, r3.at[c + 1]).wait()
        total = (rss[c // 2, 0, c % 2] + rss[c // 2, 1, c % 2]) + (rss[c // 2, 2, c % 2] + rss[c // 2, 3, c % 2])
        factor = lax.rsqrt(total * (1.0 / (CH * CHANS)) + EPS)
        for g in range(2):
            rows = pl.ds(c * LEN + g * 128, 128)
            column = jnp.transpose(jnp.broadcast_to(factor[g : g + 1, :], (128, 128)))
            for l in range(TILES):
                cols = pl.ds(l * 128, 128)
                out[rows, cols] = (near[rows, cols] * column * gain_v[:, cols]).astype(BF16)

    @pl.when(jnp.logical_not(serves))
    def _():
        pltpu.make_async_copy(send1, send1, s1).wait()

    @pl.when(serves)
    def _():
        rest = send1.at[pl.ds(0, len(SERVERS) - 1)]
        pltpu.make_async_copy(rest, rest, s1).wait()
        sent = send2.at[pl.ds(0, CTX - 1)]
        pltpu.make_async_copy(sent, sent, s2).wait()

    sent = rss.at[:, pl.ds(0, CH - 1)]
    pltpu.make_async_copy(sent, sent, s3).wait()


def local(prefix, suffix, gates, rates, residues, gain, order, blocks):
    packed, places = tables()
    hbm = pl.BlockSpec(memory_space=pltpu.HBM)
    vmem = pltpu.VMEM
    dma = pltpu.SemaphoreType.DMA
    scratch = [
        pltpu.SMEM((2 * CTX,), jnp.int32),
        vmem((6 * LEN, CHANS), BF16),
        vmem((4 * LEN, CHANS), BF16),
        vmem((4 * LEN, CHANS), F32),
        vmem((MODES, CHANS), F32),
        vmem((MODES, CHANS), F32),
        vmem((1, CHANS), F32),
        vmem((2 * ORD, LEN), BF16),
        vmem((2 * LEN, LEN), BF16),
        vmem((LEN, 2 * LEN), BF16),
        vmem((2 * LEN, 128), BF16),
        vmem((LEN, 128), BF16),
        vmem((8, 128), jnp.int32),
        pltpu.SMEM((8, 128), jnp.int32),
        vmem((128, 128), F32),
        vmem((6, 128, 128), F32),
        vmem((6, ORD, 8, 128), F32),
        vmem((MODES, ORD, 8, 128), F32),
        vmem((MODES, 8, 128), F32),
        vmem((MODES, 8, 128), F32),
        vmem((MODES, 8, 128), F32),
        vmem((MODES, 8, 128), F32),
        vmem((MODES, 8, 128), F32),
        vmem((MODES, 8, 128), F32),
        vmem((2, MODES, 8, 128), F32),
        vmem((4, 2 * LEN, 256), F32),
        vmem((4, 2 * LEN, 256), BF16),
        vmem((LEN, CHANS), F32),
        vmem((LEN, CHANS), F32),
        vmem((3 * ORD, CHANS), BF16),
        vmem((128, 128), F32),
        vmem((4, MODES, 8, 128), F32),
        vmem((4, 128, 128), F32),
        vmem((4, 3 * ORD, CHANS), BF16),
        vmem((len(SERVERS), 3, 16, 128), BF16),
        vmem((CTX, 3, 16, 128), BF16),
        vmem((2 * CTX, 16, 128), F32),
        vmem((CTX, 2, 16, 128), BF16),
        vmem((len(SERVERS), 2, 16, 128), BF16),
        vmem((4, LEN, 128), F32),
        vmem((4, 2, 128), F32),
        vmem((2, CH, 2, 2, 128), F32),
        dma((4,)),
        dma((3,)),
        dma,
        dma((len(places),)),
        dma,
        dma, dma, dma, dma, dma, dma((4,)),
    ]
    operands = (
        order, prefix, suffix, gates, rates, residues, gain[None, :], jnp.asarray(packed)
    )
    return pl.pallas_call(
        functools.partial(kernel, places),
        out_shape=pltpu.VMEM((4 * LEN, CHANS), BF16),
        in_specs=[pl.BlockSpec(memory_space=pltpu.SMEM)] + [hbm] * 8,
        out_specs=pl.BlockSpec(memory_space=pltpu.VMEM),
        scratch_shapes=scratch,
        compiler_params=pltpu.CompilerParams(
            collective_id=0, has_side_effects=True, vmem_limit_bytes=48 * 1024 * 1024
        ),
        cost_estimate=pl.CostEstimate(
            flops=6_000_000_000, bytes_accessed=8_000_000, transcendentals=100_000
        ),
    )(blocks, *(pltpu.with_memory_space_constraint(a, pltpu.HBM) for a in operands))


def solution(mesh):
    return jax.shard_map(
        local,
        mesh=mesh,
        in_specs=(
            P("ctx", "ch"),
            P("ctx", "ch"),
            P("ctx", "ch"),
            P(None, "ch"),
            P(None, "ch"),
            P("ch"),
            P(),
            P(),
        ),
        out_specs=P("ctx", "ch"),
        check_vma=False,
    )
```

```python
import functools

import jax
import jax.numpy as jnp
import ml_dtypes
import numpy as np
from jax import lax
from jax.experimental import pallas as pl
from jax.experimental.pallas import tpu as pltpu
from jax.sharding import PartitionSpec as P

MESH = pl.DeviceIdType.MESH
F32 = jnp.float32
BF16 = jnp.bfloat16

LEN = 256
ORD = 16
MODES = 16
CTX = 32
CH = 4
CHANS = 1024
TILES = CHANS // 128
RATE_HALF = 1.0 / 48.0
EPS = 1e-6


def series():
    nodes = 64
    angle = np.pi * (np.arange(nodes) + 0.5) / nodes
    rate = RATE_HALF * (1.0 + np.cos(angle))
    values = np.exp(-rate[:, None] * np.arange(LEN)[None, :])
    basis = np.cos(np.arange(ORD)[:, None] * angle[None, :])
    psi = 2.0 / nodes * (basis @ values)
    psi[0] *= 0.5
    return psi


def halves(a):
    high = a.astype(np.float32).astype(ml_dtypes.bfloat16)
    low = (a - high.astype(np.float64)).astype(np.float32).astype(ml_dtypes.bfloat16)
    return high, low


def tables():
    psi = series()
    theta = np.pi / (2 * LEN) * np.outer(2 * np.arange(LEN) + 1, np.arange(LEN))
    forward = np.concatenate([np.cos(theta), -np.sin(theta)], 0)
    inverse = np.concatenate([np.cos(theta).T, -np.sin(theta).T], 1) / LEN
    to_bf16 = lambda a: a.astype(np.float32).astype(ml_dtypes.bfloat16)
    ends = np.concatenate(halves(psi[:, ::-1]), 0)
    th, tl = halves(forward @ psi.T)
    fh, fl = halves(psi.T)
    arrays = (
        ends,
        np.concatenate([th, tl, th], 1),
        to_bf16(forward),
        to_bf16(inverse),
        np.concatenate([fh, fl, fh], 1),
    )
    slabs, places, row = [], [], 0
    for a in arrays:
        a = np.pad(a, ((0, 0), (0, -a.shape[1] % 128)))
        for col in range(0, a.shape[1], 128):
            slabs.append(a[:, col : col + 128])
            places.append((row, a.shape[0], col))
            row += a.shape[0]
    return np.concatenate(slabs, 0), places


def place_of(ctx):
    return ctx // 16, ctx // 4 % 4, ctx % 4


def lateness(ctx):
    x, z, y = place_of(ctx)
    return 1.5 * x + 1.0 * z + 0.85 * y


BY_START = sorted(range(CTX), key=lateness)
SERVERS = [0, 1, 4, 16, 2, 8, 3, 20]
PER = MODES // len(SERVERS)


def split(a):
    high = a.astype(BF16)
    low = (a - high.astype(F32)).astype(BF16)
    return high, low


def dot(a, b):
    return jnp.dot(a, b, preferred_element_type=F32)


def kernel(
    places,
    blocks, order_h, prefix, suffix, gates, rates, residues, gain, packed,
    out,
    order, x, gt, near, rate_v, res_v, gain_v,
    ends, forward, inverse, taps, fart,
    idx_v, idx_s,
    relay, zrel, zd, tt, rate_m, coef, step1, dec1, dec2, pw,
    mid, spec, prod, hr, hi, hb, grel, gm, gb, hf,
    send1, recv1, incoming, send2, recv2, acc, ss, rss,
    sem_small, sem_x, sem_gate, sem_const, sem_idx,
    s1, r1, s2, r2, s3, r3,
):
    me = lax.axis_index("ctx")
    mc = lax.axis_index("ch")

    small = [
        pltpu.make_async_copy(rates, rate_v, sem_small.at[0]),
        pltpu.make_async_copy(residues, res_v, sem_small.at[1]),
        pltpu.make_async_copy(order_h, order, sem_small.at[2]),
        pltpu.make_async_copy(gain, gain_v, sem_small.at[3]),
    ]
    targets = [ends] * 2 + [taps] + [forward] * 2 + [inverse] * 4 + [fart]
    consts = [
        pltpu.make_async_copy(
            packed.at[pl.ds(row, count)], target.at[:, pl.ds(col, 128)], sem_const.at[i]
        )
        for i, ((row, count, col), target) in enumerate(zip(places, targets))
    ]
    xcopies = [
        pltpu.make_async_copy(prefix, x.at[pl.ds(0, 2 * LEN)], sem_x.at[0]),
        pltpu.make_async_copy(
            suffix.at[pl.ds(0, 2 * LEN)], x.at[pl.ds(2 * LEN, 2 * LEN)], sem_x.at[1]
        ),
        pltpu.make_async_copy(
            suffix.at[pl.ds(2 * LEN, 2 * LEN)], x.at[pl.ds(4 * LEN, 2 * LEN)], sem_x.at[2]
        ),
    ]
    gate_copy = pltpu.make_async_copy(gates, gt, sem_gate)
    for copy in small[:1] + consts[:2] + xcopies:
        copy.start()

    barrier = pltpu.get_barrier_semaphore()
    others = [lax.rem(mc + r, CH) for r in (2, 3, 1)]
    serves = functools.reduce(jnp.logical_or, [me == ctx for ctx in SERVERS])
    number = sum(jnp.where(me == ctx, i, 0) for i, ctx in enumerate(SERVERS))
    replies = len(SERVERS) - jnp.where(serves, 1, 0)

    @pl.when(serves)
    def _():
        for to in BY_START:

            @pl.when(me != to)
            def _():
                pl.semaphore_signal(barrier, inc=1, device_id=(to, mc), device_id_type=MESH)

    for to in others:
        pl.semaphore_signal(barrier, inc=1, device_id=(me, to), device_id_type=MESH)

    small[0].wait()

    def spread(read):
        for g in range(2):
            for l in range(TILES):
                relay[pl.ds(g * 64 + l * 8, 8), :] = read(g, l)

    def mode(m):
        return relay[pl.ds(m // 8 * 64 + m % 8, 8, stride=8), :]

    live = blocks[0]
    gap = jnp.maximum(live - 1 - me, 0).astype(F32) * (2.0 * LEN)
    alive = jnp.where(me < live, 1.0, 0.0).astype(F32)
    spread(lambda g, l: rate_v[pl.ds(g * 8, 8), pl.ds(l * 128, 128)])
    for m in range(MODES):
        rate = mode(m)
        rate_m[m] = rate
        dec1[m] = jnp.exp(rate * (-1.0 * LEN))
        pw[m] = jnp.exp(rate * -gap) * alive
        s = rate * (1.0 / RATE_HALF) - 1.0
        older, newer = jnp.ones_like(s), s
        tt[m, 0] = older
        tt[m, 1] = newer
        for k in range(2, ORD):
            older, newer = newer, 2.0 * s * newer - older
            tt[m, k] = newer

    for copy in consts[:2]:
        copy.wait()
    for c in range(6):
        if c % 2 == 0:
            xcopies[c // 2].wait()
        for n in range(4):
            z = dot(ends[...], x[pl.ds(c * LEN, LEN), pl.ds(n * 256, 256)])
            z = z[:ORD] + z[ORD:]
            for g in range(2):
                for h in range(2):
                    zrel[c, pl.ds(g * 64 + (2 * n + h) * 8, 8), :] = z[
                        g * 8 : g * 8 + 8, h * 128 : h * 128 + 128
                    ]
        for k in range(ORD):
            zd[c, k] = zrel[c, pl.ds(k // 8 * 64 + k % 8, 8, stride=8), :]

    @pl.loop(0, MODES, step=4)
    def _(first):
        e = [[None] * 6 for _ in range(4)]
        for k in range(ORD):
            z = [zd[c, k] for c in range(6)]
            for i in range(4):
                t = tt[first + i, k]
                for c in range(6):
                    e[i][c] = t * z[c] if k == 0 else e[i][c] + t * z[c]
        for j in range(2):
            states = [[], [], []]
            for i in (2 * j, 2 * j + 1):
                m = first + i
                d1 = dec1[m]
                mid[0, m] = e[i][2]
                mid[1, m] = e[i][4]
                states[0].append((e[i][0] * d1 + e[i][1]) * pw[m])
                states[1].append(e[i][2] * d1 + e[i][3])
                states[2].append(e[i][4] * d1 + e[i][5])
            for q in range(3):
                send1[first // 2 + j, q] = jnp.concatenate(states[q], 0).astype(BF16)

    pl.semaphore_wait(barrier, replies + CH - 1)

    for i, to in enumerate(SERVERS):
        part = send1.at[i]

        @pl.when(me != to)
        def _():
            pltpu.make_async_remote_copy(
                src_ref=part, dst_ref=recv1.at[me], send_sem=s1, recv_sem=r1,
                device_id=(to, mc), device_id_type=MESH,
            ).start()

        @pl.when(me == to)
        def _():
            recv1[me] = part[...]

    for copy in small[1:] + consts[2:] + [gate_copy]:
        copy.start()
    for copy in small[1:]:
        copy.wait()

    lane = lax.broadcasted_iota(jnp.int32, (8, 128), 1)

    def place(s, value):
        return jnp.where(lane == order[s], s, value)

    idx_v[...] = lax.fori_loop(0, 2 * CTX, place, jnp.zeros((8, 128), jnp.int32), unroll=8)
    idx_copy = pltpu.make_async_copy(idx_v, idx_s, sem_idx)
    idx_copy.start()

    spread(lambda g, l: res_v[pl.ds(g * 8, 8), pl.ds(l * 128, 128)])
    for m in range(MODES):
        rate = rate_m[m]
        step1[m] = jnp.exp(-rate)
        d2 = jnp.exp(rate * (-2.0 * LEN))
        dec2[m] = d2
        coef[m] = jnp.sqrt(2.0 * rate) * mode(m)

    for copy in consts[2:]:
        copy.wait()

    def natural(tiles, rows):
        for l in range(TILES):
            high, low = split(tiles[pl.ds(l, ORD, stride=8), :])
            rows[:, pl.ds(l * 128, 128)] = jnp.concatenate([high, high, low], 0)

    @pl.loop(0, ORD, step=4)
    def _(first):
        total = [None] * 4
        for m in range(MODES):
            for i in range(4):
                term = tt[m, first + i] * coef[m]
                total[i] = term if m == 0 else total[i] + term
        for i in range(4):
            grel[pl.ds(pl.multiple_of((first + i) * 8, 8), 8), :] = total[i]

    natural(grel, hb)

    @pl.loop(0, 4)
    def _(n):
        cols = pl.ds(pl.multiple_of(n * 256, 256), 256)
        both = dot(taps[:, : 3 * ORD], hb[:, cols])
        hr[:, cols] = both[:LEN]
        hi[:, cols] = both[LEN:]

    def near_chunk(c):
        rows = pl.ds(pl.multiple_of(c * LEN, LEN), LEN)
        xrows = pl.ds(pl.multiple_of((c + 2) * LEN, LEN), LEN)
        cols = [pl.ds(n * 256, 256) for n in range(4)]
        low, high = pl.ds(0, LEN), pl.ds(LEN, LEN)

        def to_spectrum(n):
            spec[n] = dot(forward[...], x[xrows, cols[n]])

        to_spectrum(0)
        for n in range(4):
            if n < 3:
                to_spectrum(n + 1)
            xr, xi = spec[n, low, :], spec[n, high, :]
            tr, ti = hr[:, cols[n]], hi[:, cols[n]]
            prod[n, low, :] = (xr * tr - xi * ti).astype(BF16)
            prod[n, high, :] = (xr * ti + xi * tr).astype(BF16)
            near[rows, cols[n]] = dot(inverse[...], prod[n])

    pl.loop(0, 2)(near_chunk)

    idx_copy.wait()

    @pl.when(serves)
    def _():
        first31 = recv1.at[pl.ds(0, CTX - 1)]
        pltpu.make_async_copy(first31, first31, r1).wait()
        parts = [None] * 4
        for c in range(CTX):
            past = recv1[c, 0].astype(F32)
            parts[c % 4] = past if c < 4 else parts[c % 4] + past
        state = (parts[0] + parts[1]) + (parts[2] + parts[3])
        a = jnp.concatenate([dec2[PER * number + i] for i in range(PER)], 0)
        aa = a * a
        for j in range(CTX):
            slots = [idx_s[0, 2 * j + q] for q in range(2)]
            first, second = [
                recv1[lax.div(slot, 2), 1 + lax.rem(slot, 2)].astype(F32) for slot in slots
            ]
            incoming[2 * j] = state
            incoming[2 * j + 1] = a * state + first
            state = aa * state + (a * first + second)
        for c in range(CTX):
            for q in range(2):
                send2[c, q] = incoming[order[2 * c + q]].astype(BF16)
        for to in BY_START:

            @pl.when(me != to)
            def _():
                pltpu.make_async_remote_copy(
                    src_ref=send2.at[to], dst_ref=recv2.at[number],
                    send_sem=s2, recv_sem=r2, device_id=(to, mc), device_id_type=MESH,
                ).start()

        recv2[number] = send2[me]

    pl.loop(2, 4)(near_chunk)

    gate_copy.wait()
    @pl.when(serves)
    def _():
        rest = recv2.at[pl.ds(0, len(SERVERS) - 1)]
        pltpu.make_async_copy(rest, rest, r2).wait()

    @pl.when(jnp.logical_not(serves))
    def _():
        pltpu.make_async_copy(recv2, recv2, r2).wait()


    for i in range(len(SERVERS)):
        for q in range(2):
            both = recv2[i, q].astype(F32)
            for j in range(PER):
                m = PER * i + j
                state = both[8 * j : 8 * j + 8]
                scale = coef[m] * step1[m]
                gm[2 * q, m] = state * scale
                gm[2 * q + 1, m] = (state * dec1[m] + mid[q, m]) * scale

    @pl.loop(0, ORD, step=4)
    def _(first):
        g = [[None] * 4 for _ in range(4)]
        for m in range(MODES):
            u = [gm[c, m] for c in range(4)]
            for i in range(4):
                t = tt[m, first + i]
                for c in range(4):
                    g[i][c] = t * u[c] if m == 0 else g[i][c] + t * u[c]
        for i in range(4):
            for c in range(4):
                gb[c, pl.ds(pl.multiple_of((first + i) * 8, 8), 8), :] = g[i][c]

    for c in range(4):
        natural(gb.at[c], hf.at[c])

    ones = jnp.ones((8, 256), BF16)
    for c in range(4):
        rows = pl.ds(c * LEN, LEN)
        for n in range(4):
            cols = pl.ds(n * 256, 256)
            value = near[rows, cols] + dot(fart[:, : 3 * ORD], hf[c, :, cols])
            value = value * gt[rows, cols].astype(F32)
            near[rows, cols] = value
            square = value * value
            square = square[:, :128] + square[:, 128:]
            acc[c] = square if n == 0 else acc[c] + square
        high, low = split(acc[c])
        dims = (((1,), (1,)), ((), ()))
        halved = jnp.concatenate([high, low], 1)
        sums = lax.dot_general(ones, halved, dims, preferred_element_type=F32)
        ss[c, pl.ds(0, 1), :] = sums[:1, :128]
        ss[c, pl.ds(1, 1), :] = sums[:1, 128:]
        rss[c // 2, mc, c % 2] = ss[c]
        for to in others if c % 2 else []:
            pltpu.make_async_remote_copy(
                src_ref=ss.at[pl.ds(c - 1, 2)], dst_ref=rss.at[c // 2, mc], send_sem=s3, recv_sem=r3.at[c],
                device_id=(me, to), device_id_type=MESH,
            ).start()

    for c in range(4):
        if c % 2 == 0:
            three = rss.at[c // 2, pl.ds(0, CH - 1)]
            pltpu.make_async_copy(three, three, r3.at[c + 1]).wait()
        total = (rss[c // 2, 0, c % 2] + rss[c // 2, 1, c % 2]) + (rss[c // 2, 2, c % 2] + rss[c // 2, 3, c % 2])
        factor = lax.rsqrt(total * (1.0 / (CH * CHANS)) + EPS)
        for g in range(2):
            rows = pl.ds(c * LEN + g * 128, 128)
            column = jnp.transpose(jnp.broadcast_to(factor[g : g + 1, :], (128, 128)))
            for l in range(TILES):
                cols = pl.ds(l * 128, 128)
                out[rows, cols] = (near[rows, cols] * column * gain_v[:, cols]).astype(BF16)

    @pl.when(jnp.logical_not(serves))
    def _():
        pltpu.make_async_copy(send1, send1, s1).wait()

    @pl.when(serves)
    def _():
        rest = send1.at[pl.ds(0, len(SERVERS) - 1)]
        pltpu.make_async_copy(rest, rest, s1).wait()
        sent = send2.at[pl.ds(0, CTX - 1)]
        pltpu.make_async_copy(sent, sent, s2).wait()

    sent = rss.at[:, pl.ds(0, CH - 1)]
    pltpu.make_async_copy(sent, sent, s3).wait()


def local(prefix, suffix, gates, rates, residues, gain, order, blocks):
    packed, places = tables()
    hbm = pl.BlockSpec(memory_space=pltpu.HBM)
    vmem = pltpu.VMEM
    dma = pltpu.SemaphoreType.DMA
    scratch = [
        pltpu.SMEM((2 * CTX,), jnp.int32),
        vmem((6 * LEN, CHANS), BF16),
        vmem((4 * LEN, CHANS), BF16),
        vmem((4 * LEN, CHANS), F32),
        vmem((MODES, CHANS), F32),
        vmem((MODES, CHANS), F32),
        vmem((1, CHANS), F32),
        vmem((2 * ORD, LEN), BF16),
        vmem((2 * LEN, LEN), BF16),
        vmem((LEN, 2 * LEN), BF16),
        vmem((2 * LEN, 128), BF16),
        vmem((LEN, 128), BF16),
        vmem((8, 128), jnp.int32),
        pltpu.SMEM((8, 128), jnp.int32),
        vmem((128, 128), F32),
        vmem((6, 128, 128), F32),
        vmem((6, ORD, 8, 128), F32),
        vmem((MODES, ORD, 8, 128), F32),
        vmem((MODES, 8, 128), F32),
        vmem((MODES, 8, 128), F32),
        vmem((MODES, 8, 128), F32),
        vmem((MODES, 8, 128), F32),
        vmem((MODES, 8, 128), F32),
        vmem((MODES, 8, 128), F32),
        vmem((2, MODES, 8, 128), F32),
        vmem((4, 2 * LEN, 256), F32),
        vmem((4, 2 * LEN, 256), BF16),
        vmem((LEN, CHANS), F32),
        vmem((LEN, CHANS), F32),
        vmem((3 * ORD, CHANS), BF16),
        vmem((128, 128), F32),
        vmem((4, MODES, 8, 128), F32),
        vmem((4, 128, 128), F32),
        vmem((4, 3 * ORD, CHANS), BF16),
        vmem((len(SERVERS), 3, 16, 128), BF16),
        vmem((CTX, 3, 16, 128), BF16),
        vmem((2 * CTX, 16, 128), F32),
        vmem((CTX, 2, 16, 128), BF16),
        vmem((len(SERVERS), 2, 16, 128), BF16),
        vmem((4, LEN, 128), F32),
        vmem((4, 2, 128), F32),
        vmem((2, CH, 2, 2, 128), F32),
        dma((4,)),
        dma((3,)),
        dma,
        dma((len(places),)),
        dma,
        dma, dma, dma, dma, dma, dma((4,)),
    ]
    operands = (
        order, prefix, suffix, gates, rates, residues, gain[None, :], jnp.asarray(packed)
    )
    return pl.pallas_call(
        functools.partial(kernel, places),
        out_shape=pltpu.VMEM((4 * LEN, CHANS), BF16),
        in_specs=[pl.BlockSpec(memory_space=pltpu.SMEM)] + [hbm] * 8,
        out_specs=pl.BlockSpec(memory_space=pltpu.VMEM),
        scratch_shapes=scratch,
        compiler_params=pltpu.CompilerParams(
            collective_id=0, has_side_effects=True, vmem_limit_bytes=48 * 1024 * 1024
        ),
        cost_estimate=pl.CostEstimate(
            flops=6_000_000_000, bytes_accessed=8_000_000, transcendentals=100_000
        ),
    )(blocks, *(pltpu.with_memory_space_constraint(a, pltpu.HBM) for a in operands))


def solution(mesh):
    return jax.shard_map(
        local,
        mesh=mesh,
        in_specs=(
            P("ctx", "ch"),
            P("ctx", "ch"),
            P("ctx", "ch"),
            P(None, "ch"),
            P(None, "ch"),
            P("ch"),
            P(),
            P(),
        ),
        out_specs=P("ctx", "ch"),
        check_vma=False,
    )
```

```python
import functools

import jax
import jax.numpy as jnp
import ml_dtypes
import numpy as np
from jax import lax
from jax.experimental import pallas as pl
from jax.experimental.pallas import tpu as pltpu
from jax.sharding import PartitionSpec as P

MESH = pl.DeviceIdType.MESH
F32 = jnp.float32
BF16 = jnp.bfloat16

LEN = 256
ORD = 16
MODES = 16
CTX = 32
CH = 4
CHANS = 1024
TILES = CHANS // 128
RATE_HALF = 1.0 / 48.0
EPS = 1e-6


def series():
    nodes = 64
    angle = np.pi * (np.arange(nodes) + 0.5) / nodes
    rate = RATE_HALF * (1.0 + np.cos(angle))
    values = np.exp(-rate[:, None] * np.arange(LEN)[None, :])
    basis = np.cos(np.arange(ORD)[:, None] * angle[None, :])
    psi = 2.0 / nodes * (basis @ values)
    psi[0] *= 0.5
    return psi


def halves(a):
    high = a.astype(np.float32).astype(ml_dtypes.bfloat16)
    low = (a - high.astype(np.float64)).astype(np.float32).astype(ml_dtypes.bfloat16)
    return high, low


def tables():
    psi = series()
    theta = np.pi / (2 * LEN) * np.outer(2 * np.arange(LEN) + 1, np.arange(LEN))
    forward = np.concatenate([np.cos(theta), -np.sin(theta)], 0)
    inverse = np.concatenate([np.cos(theta).T, -np.sin(theta).T], 1) / LEN
    to_bf16 = lambda a: a.astype(np.float32).astype(ml_dtypes.bfloat16)
    ends = np.concatenate(halves(psi[:, ::-1]), 0)
    th, tl = halves(forward @ psi.T)
    fh, fl = halves(psi.T)
    arrays = (
        ends,
        np.concatenate([th, tl, th], 1),
        to_bf16(forward),
        to_bf16(inverse),
        np.concatenate([fh, fl, fh], 1),
    )
    slabs, places, row = [], [], 0
    for a in arrays:
        a = np.pad(a, ((0, 0), (0, -a.shape[1] % 128)))
        for col in range(0, a.shape[1], 128):
            slabs.append(a[:, col : col + 128])
            places.append((row, a.shape[0], col))
            row += a.shape[0]
    return np.concatenate(slabs, 0), places


def place_of(ctx):
    return ctx // 16, ctx // 4 % 4, ctx % 4


def lateness(ctx):
    x, z, y = place_of(ctx)
    return 1.5 * x + 1.0 * z + 0.85 * y


BY_START = sorted(range(CTX), key=lateness)
SERVERS = [0, 1, 4, 16, 2, 8, 3, 20]
PER = MODES // len(SERVERS)


def split(a):
    high = a.astype(BF16)
    low = (a - high.astype(F32)).astype(BF16)
    return high, low


def dot(a, b):
    return jnp.dot(a, b, preferred_element_type=F32)


def kernel(
    places,
    blocks, order_h, prefix, suffix, gates, rates, residues, gain, packed,
    out,
    order, x, gt, near, rate_v, res_v, gain_v,
    ends, forward, inverse, taps, fart,
    idx_v, idx_s,
    relay, zrel, zd, tt, rate_m, coef, step1, dec1, dec2, pw,
    mid, spec, prod, hr, hi, hb, grel, gm, gb, hf,
    send1, recv1, incoming, send2, recv2, acc, ss, rss,
    sem_small, sem_x, sem_gate, sem_const, sem_idx,
    s1, r1, s2, r2, s3, r3,
):
    me = lax.axis_index("ctx")
    mc = lax.axis_index("ch")

    small = [
        pltpu.make_async_copy(rates, rate_v, sem_small.at[0]),
        pltpu.make_async_copy(residues, res_v, sem_small.at[1]),
        pltpu.make_async_copy(order_h, order, sem_small.at[2]),
        pltpu.make_async_copy(gain, gain_v, sem_small.at[3]),
    ]
    targets = [ends] * 2 + [taps] + [forward] * 2 + [inverse] * 4 + [fart]
    consts = [
        pltpu.make_async_copy(
            packed.at[pl.ds(row, count)], target.at[:, pl.ds(col, 128)], sem_const.at[i]
        )
        for i, ((row, count, col), target) in enumerate(zip(places, targets))
    ]
    xcopies = [
        pltpu.make_async_copy(prefix, x.at[pl.ds(0, 2 * LEN)], sem_x.at[0]),
        pltpu.make_async_copy(
            suffix.at[pl.ds(0, 2 * LEN)], x.at[pl.ds(2 * LEN, 2 * LEN)], sem_x.at[1]
        ),
        pltpu.make_async_copy(
            suffix.at[pl.ds(2 * LEN, 2 * LEN)], x.at[pl.ds(4 * LEN, 2 * LEN)], sem_x.at[2]
        ),
    ]
    gate_copy = pltpu.make_async_copy(gates, gt, sem_gate)
    for copy in small[:1] + consts[:2] + xcopies:
        copy.start()

    barrier = pltpu.get_barrier_semaphore()
    others = [lax.rem(mc + r, CH) for r in (2, 3, 1)]
    serves = functools.reduce(jnp.logical_or, [me == ctx for ctx in SERVERS])
    number = sum(jnp.where(me == ctx, i, 0) for i, ctx in enumerate(SERVERS))
    replies = len(SERVERS) - jnp.where(serves, 1, 0)

    @pl.when(serves)
    def _():
        for to in BY_START:

            @pl.when(me != to)
            def _():
                pl.semaphore_signal(barrier, inc=1, device_id=(to, mc), device_id_type=MESH)

    for to in others:
        pl.semaphore_signal(barrier, inc=1, device_id=(me, to), device_id_type=MESH)

    small[0].wait()

    def spread(read):
        for g in range(2):
            for l in range(TILES):
                relay[pl.ds(g * 64 + l * 8, 8), :] = read(g, l)

    def mode(m):
        return relay[pl.ds(m // 8 * 64 + m % 8, 8, stride=8), :]

    live = blocks[0]
    gap = jnp.maximum(live - 1 - me, 0).astype(F32) * (2.0 * LEN)
    alive = jnp.where(me < live, 1.0, 0.0).astype(F32)
    spread(lambda g, l: rate_v[pl.ds(g * 8, 8), pl.ds(l * 128, 128)])
    for m in range(MODES):
        rate = mode(m)
        rate_m[m] = rate
        dec1[m] = jnp.exp(rate * (-1.0 * LEN))
        pw[m] = jnp.exp(rate * -gap) * alive
        s = rate * (1.0 / RATE_HALF) - 1.0
        older, newer = jnp.ones_like(s), s
        tt[m, 0] = older
        tt[m, 1] = newer
        for k in range(2, ORD):
            older, newer = newer, 2.0 * s * newer - older
            tt[m, k] = newer

    for copy in consts[:2]:
        copy.wait()
    for c in range(6):
        if c % 2 == 0:
            xcopies[c // 2].wait()
        for n in range(4):
            z = dot(ends[...], x[pl.ds(c * LEN, LEN), pl.ds(n * 256, 256)])
            z = z[:ORD] + z[ORD:]
            for g in range(2):
                for h in range(2):
                    zrel[c, pl.ds(g * 64 + (2 * n + h) * 8, 8), :] = z[
                        g * 8 : g * 8 + 8, h * 128 : h * 128 + 128
                    ]
        for k in range(ORD):
            zd[c, k] = zrel[c, pl.ds(k // 8 * 64 + k % 8, 8, stride=8), :]

    @pl.loop(0, MODES, step=4)
    def _(first):
        e = [[None] * 6 for _ in range(4)]
        for k in range(ORD):
            z = [zd[c, k] for c in range(6)]
            for i in range(4):
                t = tt[first + i, k]
                for c in range(6):
                    e[i][c] = t * z[c] if k == 0 else e[i][c] + t * z[c]
        for j in range(2):
            states = [[], [], []]
            for i in (2 * j, 2 * j + 1):
                m = first + i
                d1 = dec1[m]
                mid[0, m] = e[i][2]
                mid[1, m] = e[i][4]
                states[0].append((e[i][0] * d1 + e[i][1]) * pw[m])
                states[1].append(e[i][2] * d1 + e[i][3])
                states[2].append(e[i][4] * d1 + e[i][5])
            for q in range(3):
                send1[first // 2 + j, q] = jnp.concatenate(states[q], 0).astype(BF16)

    pl.semaphore_wait(barrier, replies + CH - 1)

    for i, to in enumerate(SERVERS):
        part = send1.at[i]

        @pl.when(me != to)
        def _():
            pltpu.make_async_remote_copy(
                src_ref=part, dst_ref=recv1.at[me], send_sem=s1, recv_sem=r1,
                device_id=(to, mc), device_id_type=MESH,
            ).start()

        @pl.when(me == to)
        def _():
            recv1[me] = part[...]

    for copy in small[1:] + consts[2:] + [gate_copy]:
        copy.start()
    for copy in small[1:]:
        copy.wait()

    lane = lax.broadcasted_iota(jnp.int32, (8, 128), 1)

    def place(s, value):
        return jnp.where(lane == order[s], s, value)

    idx_v[...] = lax.fori_loop(0, 2 * CTX, place, jnp.zeros((8, 128), jnp.int32), unroll=8)
    idx_copy = pltpu.make_async_copy(idx_v, idx_s, sem_idx)
    idx_copy.start()

    spread(lambda g, l: res_v[pl.ds(g * 8, 8), pl.ds(l * 128, 128)])
    for m in range(MODES):
        rate = rate_m[m]
        step1[m] = jnp.exp(-rate)
        d2 = jnp.exp(rate * (-2.0 * LEN))
        dec2[m] = d2
        coef[m] = jnp.sqrt(2.0 * rate) * mode(m)

    for copy in consts[2:]:
        copy.wait()

    def natural(tiles, rows):
        for l in range(TILES):
            high, low = split(tiles[pl.ds(l, ORD, stride=8), :])
            rows[:, pl.ds(l * 128, 128)] = jnp.concatenate([high, high, low], 0)

    @pl.loop(0, ORD, step=4)
    def _(first):
        total = [None] * 4
        for m in range(MODES):
            for i in range(4):
                term = tt[m, first + i] * coef[m]
                total[i] = term if m == 0 else total[i] + term
        for i in range(4):
            grel[pl.ds(pl.multiple_of((first + i) * 8, 8), 8), :] = total[i]

    natural(grel, hb)

    @pl.loop(0, 4)
    def _(n):
        cols = pl.ds(pl.multiple_of(n * 256, 256), 256)
        both = dot(taps[:, : 3 * ORD], hb[:, cols])
        hr[:, cols] = both[:LEN]
        hi[:, cols] = both[LEN:]

    def near_chunk(c):
        rows = pl.ds(pl.multiple_of(c * LEN, LEN), LEN)
        xrows = pl.ds(pl.multiple_of((c + 2) * LEN, LEN), LEN)
        cols = [pl.ds(n * 256, 256) for n in range(4)]
        low, high = pl.ds(0, LEN), pl.ds(LEN, LEN)

        def to_spectrum(n):
            spec[n] = dot(forward[...], x[xrows, cols[n]])

        to_spectrum(0)
        for n in range(4):
            if n < 3:
                to_spectrum(n + 1)
            xr, xi = spec[n, low, :], spec[n, high, :]
            tr, ti = hr[:, cols[n]], hi[:, cols[n]]
            prod[n, low, :] = (xr * tr - xi * ti).astype(BF16)
            prod[n, high, :] = (xr * ti + xi * tr).astype(BF16)
            near[rows, cols[n]] = dot(inverse[...], prod[n])

    pl.loop(0, 2)(near_chunk)

    idx_copy.wait()

    @pl.when(serves)
    def _():
        first31 = recv1.at[pl.ds(0, CTX - 1)]
        pltpu.make_async_copy(first31, first31, r1).wait()
        parts = [None] * 4
        for c in range(CTX):
            past = recv1[c, 0].astype(F32)
            parts[c % 4] = past if c < 4 else parts[c % 4] + past
        state = (parts[0] + parts[1]) + (parts[2] + parts[3])
        a = jnp.concatenate([dec2[PER * number + i] for i in range(PER)], 0)
        aa = a * a
        for j in range(CTX):
            slots = [idx_s[0, 2 * j + q] for q in range(2)]
            first, second = [
                recv1[lax.div(slot, 2), 1 + lax.rem(slot, 2)].astype(F32) for slot in slots
            ]
            incoming[2 * j] = state
            incoming[2 * j + 1] = a * state + first
            state = aa * state + (a * first + second)
        for c in range(CTX):
            for q in range(2):
                send2[c, q] = incoming[order[2 * c + q]].astype(BF16)
        for to in BY_START:

            @pl.when(me != to)
            def _():
                pltpu.make_async_remote_copy(
                    src_ref=send2.at[to], dst_ref=recv2.at[number],
                    send_sem=s2, recv_sem=r2, device_id=(to, mc), device_id_type=MESH,
                ).start()

        recv2[number] = send2[me]

    pl.loop(2, 4)(near_chunk)

    gate_copy.wait()
    @pl.when(serves)
    def _():
        rest = recv2.at[pl.ds(0, len(SERVERS) - 1)]
        pltpu.make_async_copy(rest, rest, r2).wait()

    @pl.when(jnp.logical_not(serves))
    def _():
        pltpu.make_async_copy(recv2, recv2, r2).wait()


    for i in range(len(SERVERS)):
        for q in range(2):
            both = recv2[i, q].astype(F32)
            for j in range(PER):
                m = PER * i + j
                state = both[8 * j : 8 * j + 8]
                scale = coef[m] * step1[m]
                gm[2 * q, m] = state * scale
                gm[2 * q + 1, m] = (state * dec1[m] + mid[q, m]) * scale

    @pl.loop(0, ORD, step=4)
    def _(first):
        g = [[None] * 4 for _ in range(4)]
        for m in range(MODES):
            u = [gm[c, m] for c in range(4)]
            for i in range(4):
                t = tt[m, first + i]
                for c in range(4):
                    g[i][c] = t * u[c] if m == 0 else g[i][c] + t * u[c]
        for i in range(4):
            for c in range(4):
                gb[c, pl.ds(pl.multiple_of((first + i) * 8, 8), 8), :] = g[i][c]

    for c in range(4):
        natural(gb.at[c], hf.at[c])

    ones = jnp.ones((8, 256), BF16)
    for c in range(4):
        rows = pl.ds(c * LEN, LEN)
        for n in range(4):
            cols = pl.ds(n * 256, 256)
            value = near[rows, cols] + dot(fart[:, : 3 * ORD], hf[c, :, cols])
            value = value * gt[rows, cols].astype(F32)
            near[rows, cols] = value * gain_v[:, cols]
            square = value * value
            square = square[:, :128] + square[:, 128:]
            acc[c] = square if n == 0 else acc[c] + square
        high, low = split(acc[c])
        dims = (((1,), (1,)), ((), ()))
        halved = jnp.concatenate([high, low], 1)
        sums = lax.dot_general(ones, halved, dims, preferred_element_type=F32)
        ss[c, pl.ds(0, 1), :] = sums[:1, :128]
        ss[c, pl.ds(1, 1), :] = sums[:1, 128:]
        rss[c // 2, mc, c % 2] = ss[c]
        for to in others if c % 2 else []:
            pltpu.make_async_remote_copy(
                src_ref=ss.at[pl.ds(c - 1, 2)], dst_ref=rss.at[c // 2, mc], send_sem=s3, recv_sem=r3.at[c],
                device_id=(me, to), device_id_type=MESH,
            ).start()

    for c in range(4):
        if c % 2 == 0:
            three = rss.at[c // 2, pl.ds(0, CH - 1)]
            pltpu.make_async_copy(three, three, r3.at[c + 1]).wait()
        total = (rss[c // 2, 0, c % 2] + rss[c // 2, 1, c % 2]) + (rss[c // 2, 2, c % 2] + rss[c // 2, 3, c % 2])
        factor = lax.rsqrt(total * (1.0 / (CH * CHANS)) + EPS)
        for g in range(2):
            rows = pl.ds(c * LEN + g * 128, 128)
            column = jnp.transpose(jnp.broadcast_to(factor[g : g + 1, :], (128, 128)))
            for l in range(TILES):
                cols = pl.ds(l * 128, 128)
                out[rows, cols] = (near[rows, cols] * column).astype(BF16)

    @pl.when(jnp.logical_not(serves))
    def _():
        pltpu.make_async_copy(send1, send1, s1).wait()

    @pl.when(serves)
    def _():
        rest = send1.at[pl.ds(0, len(SERVERS) - 1)]
        pltpu.make_async_copy(rest, rest, s1).wait()
        sent = send2.at[pl.ds(0, CTX - 1)]
        pltpu.make_async_copy(sent, sent, s2).wait()

    sent = rss.at[:, pl.ds(0, CH - 1)]
    pltpu.make_async_copy(sent, sent, s3).wait()


def local(prefix, suffix, gates, rates, residues, gain, order, blocks):
    packed, places = tables()
    hbm = pl.BlockSpec(memory_space=pltpu.HBM)
    vmem = pltpu.VMEM
    dma = pltpu.SemaphoreType.DMA
    scratch = [
        pltpu.SMEM((2 * CTX,), jnp.int32),
        vmem((6 * LEN, CHANS), BF16),
        vmem((4 * LEN, CHANS), BF16),
        vmem((4 * LEN, CHANS), F32),
        vmem((MODES, CHANS), F32),
        vmem((MODES, CHANS), F32),
        vmem((1, CHANS), F32),
        vmem((2 * ORD, LEN), BF16),
        vmem((2 * LEN, LEN), BF16),
        vmem((LEN, 2 * LEN), BF16),
        vmem((2 * LEN, 128), BF16),
        vmem((LEN, 128), BF16),
        vmem((8, 128), jnp.int32),
        pltpu.SMEM((8, 128), jnp.int32),
        vmem((128, 128), F32),
        vmem((6, 128, 128), F32),
        vmem((6, ORD, 8, 128), F32),
        vmem((MODES, ORD, 8, 128), F32),
        vmem((MODES, 8, 128), F32),
        vmem((MODES, 8, 128), F32),
        vmem((MODES, 8, 128), F32),
        vmem((MODES, 8, 128), F32),
        vmem((MODES, 8, 128), F32),
        vmem((MODES, 8, 128), F32),
        vmem((2, MODES, 8, 128), F32),
        vmem((4, 2 * LEN, 256), F32),
        vmem((4, 2 * LEN, 256), BF16),
        vmem((LEN, CHANS), F32),
        vmem((LEN, CHANS), F32),
        vmem((3 * ORD, CHANS), BF16),
        vmem((128, 128), F32),
        vmem((4, MODES, 8, 128), F32),
        vmem((4, 128, 128), F32),
        vmem((4, 3 * ORD, CHANS), BF16),
        vmem((len(SERVERS), 3, 16, 128), BF16),
        vmem((CTX, 3, 16, 128), BF16),
        vmem((2 * CTX, 16, 128), F32),
        vmem((CTX, 2, 16, 128), BF16),
        vmem((len(SERVERS), 2, 16, 128), BF16),
        vmem((4, LEN, 128), F32),
        vmem((4, 2, 128), F32),
        vmem((2, CH, 2, 2, 128), F32),
        dma((4,)),
        dma((3,)),
        dma,
        dma((len(places),)),
        dma,
        dma, dma, dma, dma, dma, dma((4,)),
    ]
    operands = (
        order, prefix, suffix, gates, rates, residues, gain[None, :], jnp.asarray(packed)
    )
    return pl.pallas_call(
        functools.partial(kernel, places),
        out_shape=pltpu.VMEM((4 * LEN, CHANS), BF16),
        in_specs=[pl.BlockSpec(memory_space=pltpu.SMEM)] + [hbm] * 8,
        out_specs=pl.BlockSpec(memory_space=pltpu.VMEM),
        scratch_shapes=scratch,
        compiler_params=pltpu.CompilerParams(
            collective_id=0, has_side_effects=True, vmem_limit_bytes=48 * 1024 * 1024
        ),
        cost_estimate=pl.CostEstimate(
            flops=6_000_000_000, bytes_accessed=8_000_000, transcendentals=100_000
        ),
    )(blocks, *(pltpu.with_memory_space_constraint(a, pltpu.HBM) for a in operands))


def solution(mesh):
    return jax.shard_map(
        local,
        mesh=mesh,
        in_specs=(
            P("ctx", "ch"),
            P("ctx", "ch"),
            P("ctx", "ch"),
            P(None, "ch"),
            P(None, "ch"),
            P("ch"),
            P(),
            P(),
        ),
        out_specs=P("ctx", "ch"),
        check_vma=False,
    )
```
